256 devices in a mesh: batch: 32 (over x, z), head: 8 (over y, core).
Axes of the slice: x: 4, y: 4, z: 8, core: 2. Of those that a mesh axis runs over, the one named last changes fastest.
Arguments:
- resid_in: bfloat16 [16384, 2304], P('batch', 'head'), may hold values from -40 to 40
- kda_q: bfloat16 [16384, 4096], P('batch', 'head'), may hold values from -6 to 6
- kda_k: bfloat16 [16384, 4096], P('batch', 'head'), may hold values from -6 to 6
- kda_v: bfloat16 [16384, 4096], P('batch', 'head'), may hold values from -6 to 6
- log_decay: float32 [16384, 4096], P('batch', 'head'), may hold values from -1 to 0
- beta: float32 [16384, 32], P('batch', 'head'), may hold values from 0.1 to 0.9
- out_gate: bfloat16 [16384, 4096], P('batch', 'head'), may hold values from -6 to 6
- kda_gain: float32 [128], replicated, may hold values from 0.25 to 1.75
- kda_state: float32 [32, 32, 128, 128], P('batch', 'head'), may hold values from -4 to 4
- w_out_kda: bfloat16 [4096, 2304], P('head'), may hold values from -0.09375 to 0.09375
- mla_gain: float32 [2304], replicated, may hold values from 0.25 to 1.75
- w_q: bfloat16 [2304, 4096], P(None, 'head'), may hold values from -0.125 to 0.125
- w_uk: bfloat16 [32, 128, 512], P('head'), may hold values from -6 to 6
- w_dkv: bfloat16 [2304, 512], replicated, may hold values from -0.125 to 0.125
- latent_gain: float32 [512], replicated, may hold values from 0.25 to 1.75
- latent_pool: bfloat16 [256, 64, 512], P('batch'), may hold values from -10 to 10
- page_owner: int32 [32, 32], replicated, may hold values from 0 to 31, as said below
- page_slot: int32 [32, 32], replicated, may hold values from 0 to 7
- cached_len: int32 [32], P('batch'), may hold values from 1 to 2048, as said below
- new_len: int32 [32], P('batch'), may hold values from 1 to 512, as said below
- w_uv: bfloat16 [32, 512, 128], P('head'), may hold values from -0.25 to 0.25
Outputs:
- resid_mid: bfloat16 [16384, 2304], P('batch', 'head')
- kda_state_out: float32 [32, 32, 128, 128], P('batch', 'head')
- mla_out: bfloat16 [16384, 4096], P('batch', 'head')
The draws below stay inside these ranges and needn't reach their ends.
Inputs may be any that keep to these rules, and one draw needn't show every extreme that they name: `page_owner`: in one session's row no owner appears more than 2 times; one owner, the same for every session, appears exactly 2 times in every row. `cached_len`: some session holds exactly 2048 cached tokens. `new_len`: some session has exactly 512 new tokens.
All inputs are finite; a program needn't handle non-finite values.
Results may differ from the reference program's by a relative error of at most 0.035.
Values may be sent and summed in bfloat16 or wider, within the bound.
No kernel may reach another device: no remote copies, remote signals or barrier semaphores. Data moves between devices by JAX's collectives and lax.ppermute only.
A program may use at most 128 MiB of HBM per device.

```python
import math
import jax
import jax.numpy as jnp
from jax import lax

D = 2304
HEADS = 32
HD = 128
LAT = 512
FRESH_SLOTS = 512
PAGES = 32
PAGE = 64
SESSION_COUNT = 32
POOL_OWNERS = 32
TOKENS = 16384
HK = 4096
CACHE = 2048
MOST = 2
POOL_DEV = 8
POOL_TOTAL = 256


def draw_resid_in(key, part):
    key = jax.random.fold_in(key, 5)
    row_key, col_key, base_key = jax.random.split(key, 3)
    row_scale = jnp.exp(jax.random.uniform(row_key, (TOKENS, 1), minval=math.log(0.3), maxval=math.log(3.0)))
    base = jax.random.truncated_normal(base_key, -4.0, 4.0, (TOKENS, D))
    ramp = jnp.arange(D, dtype=jnp.float32) / D
    col_scale = jnp.exp(math.log(10.0) * (0.5 * ramp[None, :] + 0.5 * jax.random.uniform(col_key, (1, D))))
    return (0.25 * row_scale * col_scale * base).astype(jnp.bfloat16)


def draw_log_decay(key, part):
    key = jax.random.fold_in(key, 6)
    decay_rate_key, session_seed_key, random_noise_key, spike_seed_key, decay_depth_key = jax.random.split(key, 5)
    lower_decay_rate, upper_decay_rate, spike_gentle, spike_intense = (1.0 / 2000.0, 1.0 / 15.0, 0.8, 0.5)
    decay_rates = jnp.exp(jax.random.uniform(decay_rate_key, (SESSION_COUNT, 1, HK), minval=math.log(lower_decay_rate), maxval=math.log(upper_decay_rate)))
    multiplier = jnp.exp(jax.random.uniform(session_seed_key, (SESSION_COUNT, 1, 1), minval=math.log(0.5), maxval=math.log(2.0)))
    random_noise = jax.random.uniform(random_noise_key, (SESSION_COUNT, FRESH_SLOTS, HK), minval=0.5, maxval=1.5)
    spike_values = (jax.random.uniform(spike_seed_key, (SESSION_COUNT, FRESH_SLOTS, 1)) < 3.0 / FRESH_SLOTS).astype(jnp.float32)
    decay_depth = jax.random.uniform(decay_depth_key, (SESSION_COUNT, FRESH_SLOTS, 1), minval=math.log(spike_intense), maxval=math.log(spike_gentle))
    final_output = -decay_rates * multiplier * random_noise + spike_values * decay_depth
    return final_output.reshape(TOKENS, HK).astype(jnp.float32)


def draw_w_uk(key, part):
    key = jax.random.fold_in(key, 11)
    base_key = jax.random.fold_in(key, 0)
    final_output = jax.random.truncated_normal(base_key, -4.0, 4.0, (HEADS, HD, LAT)) / math.sqrt(HD)
    return final_output.astype(jnp.bfloat16)


def draw_latent_pool(key, part):
    key = jax.random.fold_in(key, 8)
    scale_key, base_key = jax.random.split(key, 2)
    page_scale = jnp.exp(jax.random.uniform(scale_key, (POOL_TOTAL, 1, 1), minval=math.log(0.5), maxval=math.log(2.0)))
    base = jax.random.truncated_normal(base_key, -4.0, 4.0, (POOL_TOTAL, PAGE, LAT))
    final_output = page_scale * base
    return final_output.astype(jnp.bfloat16)


def draw_page_owner(key, part):
    key = jax.random.fold_in(key, 7)
    hot_key, slot_key, order_key = jax.random.split(key, 3)
    slot_count = POOL_OWNERS * MOST
    slot_index = jnp.arange(slot_count, dtype=jnp.int32)
    slot_owner = slot_index // MOST
    hot_owner = jax.random.randint(hot_key, (), 0, POOL_OWNERS)
    scores = jax.random.randint(slot_key, (SESSION_COUNT, slot_count), 0, 1 << 20) * slot_count + slot_index[None, :]
    scores = jnp.where(slot_owner[None, :] == hot_owner, slot_index[None, :] - slot_count, scores)
    chosen = jnp.argsort(scores, axis=1)[:, :PAGES]
    owners = slot_owner[chosen]
    shuffle = jax.random.randint(order_key, (SESSION_COUNT, PAGES), 0, 1 << 20) * PAGES + jnp.arange(PAGES, dtype=jnp.int32)[None, :]
    placing = jnp.argsort(shuffle, axis=1)
    return jnp.take_along_axis(owners, placing, axis=1).astype(jnp.int32)


def draw_cached_len(key, part):
    key = jax.random.fold_in(key, 9)
    value_key, pick_key = jax.random.split(key, 2)
    lengths = jax.random.randint(value_key, (SESSION_COUNT,), 1, CACHE + 1)
    chosen = jax.random.randint(pick_key, (), 0, SESSION_COUNT)
    return jnp.where(jnp.arange(SESSION_COUNT, dtype=jnp.int32) == chosen, CACHE, lengths).astype(jnp.int32)


def draw_new_len(key, part):
    key = jax.random.fold_in(key, 13)
    value_key, pick_key = jax.random.split(key, 2)
    lengths = jax.random.randint(value_key, (SESSION_COUNT,), 1, FRESH_SLOTS + 1)
    chosen = jax.random.randint(pick_key, (), 0, SESSION_COUNT)
    return jnp.where(jnp.arange(SESSION_COUNT, dtype=jnp.int32) == chosen, FRESH_SLOTS, lengths).astype(jnp.int32)


def with_ends(drawn, stream_key, least, top_value):
    extent = drawn.shape
    index_at = [jax.random.randint(jax.random.fold_in(stream_key, axis), (), 0, extent[axis]) for axis in range(len(extent))]
    drawn = drawn.at[tuple(index_at)].set(least)
    longest = extent.index(max(extent))
    index_at[longest] = (index_at[longest] + 1) % extent[longest]
    return drawn.at[tuple(index_at)].set(top_value)


def levels(rng, dims, shards, low, top_value):
    factor_of, own = 1.0, jax.random.fold_in(rng, 6)
    for axis_at, shards_of in shards:
        heights = jnp.exp(jax.random.uniform(jax.random.fold_in(own, axis_at), (shards_of,), jnp.float32, low / len(shards), top_value / len(shards)))
        factor_of = factor_of * jnp.repeat(heights, dims[axis_at] // shards_of).reshape([-1 if axis == axis_at else 1 for axis in range(len(dims))])
    return factor_of


def normal_values(key, shape, scale, reach, shards=(), kind=jnp.bfloat16):
    values = scale * jax.random.normal(key, shape, jnp.float32)
    if shards:
        values = values * levels(key, shape, shards, -0.22, 0.18)
    return jnp.clip(values, -reach, reach).astype(kind)


def setup_inputs(seed: int = 0) -> dict:
    key_list = jax.random.split(jax.random.key(seed), 22)
    resid_in = draw_resid_in(jax.random.fold_in(key_list[21], 71), 0)
    kda_q = normal_values(key_list[1], (TOKENS, HK), 1.0, 6.0, ((0, 32), (1, 8)))
    kda_k = normal_values(key_list[2], (TOKENS, HK), 1.0, 6.0, ((0, 32), (1, 8)))
    kda_v = normal_values(key_list[3], (TOKENS, HK), 1.0, 6.0, ((0, 32), (1, 8)))
    log_decay = draw_log_decay(jax.random.fold_in(key_list[21], 71), 0)
    beta = jnp.clip(0.1 + 0.79999997 * jax.random.uniform(key_list[5], (TOKENS, HEADS), jnp.float32) ** levels(key_list[5], (TOKENS, HEADS), ((0, 32), (1, 8)), -0.2, 0.2), 0.1, 0.9)
    out_gate = normal_values(key_list[6], (TOKENS, HK), 1.0, 6.0, ((0, 32), (1, 8)))
    kda_gain = jnp.clip(1.0 + 0.15 * jax.random.normal(key_list[7], (HD,), jnp.float32), 0.25, 1.75)
    kda_state = normal_values(key_list[8], (SESSION_COUNT, HEADS, HD, HD), 0.3, 4.0, ((0, 32), (1, 8)), jnp.float32)
    w_out_kda = normal_values(key_list[9], (HK, D), HK ** -0.5, 0.09375, ((0, 8),))
    mla_gain = jnp.clip(1.0 + 0.15 * jax.random.normal(key_list[10], (D,), jnp.float32), 0.25, 1.75)
    w_q = normal_values(key_list[11], (D, HK), D ** -0.5, 0.125, ((1, 8),))
    w_uk = draw_w_uk(jax.random.fold_in(key_list[21], 71), 0)
    w_dkv = normal_values(key_list[13], (D, LAT), D ** -0.5, 0.125)
    latent_gain = jnp.clip(1.0 + 0.15 * jax.random.normal(key_list[14], (LAT,), jnp.float32), 0.25, 1.75)
    latent_pool = draw_latent_pool(jax.random.fold_in(key_list[21], 71), 0)
    page_owner = draw_page_owner(jax.random.fold_in(key_list[21], 71), 0)
    page_slot = with_ends(jax.random.randint(key_list[17], (SESSION_COUNT, PAGES), 0, POOL_DEV), jax.random.fold_in(key_list[17], 1), 0, POOL_DEV - 1).astype(jnp.int32)
    cached_len = draw_cached_len(jax.random.fold_in(key_list[21], 71), 0)
    new_len = draw_new_len(jax.random.fold_in(key_list[21], 71), 0)
    w_uv = normal_values(key_list[20], (HEADS, LAT, HD), LAT ** -0.5, 0.25, ((0, 8),))
    return {"resid_in": resid_in, "kda_q": kda_q, "kda_k": kda_k, "kda_v": kda_v, "log_decay": log_decay, "beta": beta, "out_gate": out_gate, "kda_gain": kda_gain, "kda_state": kda_state, "w_out_kda": w_out_kda, "mla_gain": mla_gain, "w_q": w_q, "w_uk": w_uk, "w_dkv": w_dkv, "latent_gain": latent_gain, "latent_pool": latent_pool, "page_owner": page_owner, "page_slot": page_slot, "cached_len": cached_len, "new_len": new_len, "w_uv": w_uv}


epsilon = 1e-06
exact_mode = lax.Precision.HIGHEST

def unit_rows(values):
    return values * lax.rsqrt(lax.optimization_barrier(jnp.sum(values * values, axis=-1, keepdims=True)) + epsilon)

def heads_view(array):
    return array.astype(jnp.float32).reshape(SESSION_COUNT, FRESH_SLOTS, HEADS, HD)

def time_major(array):
    return jnp.moveaxis(array, 1, 0)

def token_step(carried, inputs):
    query_t, key_t, value_t, decay_t, beta_t = inputs
    carried = carried * jnp.exp(decay_t)[..., None]
    recalled = jnp.einsum('shcd,shc->shd', carried, key_t, precision=exact_mode)
    update = beta_t[..., None] * (value_t - recalled)
    carried = carried + key_t[..., None] * update[..., None, :]
    return (carried, jnp.einsum('shcd,shc->shd', carried, query_t, precision=exact_mode))

def reference(resid_in, kda_q, kda_k, kda_v, log_decay, beta, out_gate, kda_gain, kda_state, w_out_kda, mla_gain, w_q, w_uk, w_dkv, latent_gain, latent_pool, page_owner, page_slot, cached_len, new_len, w_uv):
    live = (jnp.arange(FRESH_SLOTS, dtype=jnp.int32)[None, :] < new_len[:, None]).astype(jnp.float32)
    unit_q = unit_rows(heads_view(kda_q)) / math.sqrt(HD)
    unit_k = unit_rows(heads_view(kda_k))
    values = heads_view(kda_v)
    decay_live = log_decay.reshape(SESSION_COUNT, FRESH_SLOTS, HEADS, HD) * live[:, :, None, None]
    beta_live = beta.reshape(SESSION_COUNT, FRESH_SLOTS, HEADS) * live[:, :, None]
    final_state, kda_o = lax.scan(token_step, kda_state, (time_major(unit_q), time_major(unit_k), time_major(values), time_major(decay_live), time_major(beta_live)))
    kda_o = time_major(kda_o)
    scale = lax.rsqrt(lax.optimization_barrier(jnp.mean(kda_o * kda_o, axis=-1, keepdims=True)) + epsilon)
    gate = jax.nn.sigmoid(heads_view(out_gate))
    kda_mixed = (kda_o * scale * kda_gain * gate * live[:, :, None, None]).reshape(TOKENS, HK).astype(jnp.bfloat16)
    branch = jnp.dot(kda_mixed, w_out_kda, preferred_element_type=jnp.float32)
    resid_mid = (resid_in.astype(jnp.float32) + branch).astype(jnp.bfloat16)
    resid_wide = resid_mid.astype(jnp.float32)
    power = lax.optimization_barrier(jnp.mean(resid_wide * resid_wide, axis=1, keepdims=True))
    normed = (resid_wide * lax.rsqrt(power + epsilon) * mla_gain).astype(jnp.bfloat16)
    query = jnp.dot(normed, w_q, preferred_element_type=jnp.float32).astype(jnp.bfloat16)
    absorbed = jnp.einsum('tnh,nhl->tnl', query.reshape(TOKENS, HEADS, HD).astype(jnp.float32), w_uk.astype(jnp.float32), precision=exact_mode)
    absorbed = (absorbed / math.sqrt(HD)).astype(jnp.bfloat16)
    latent_pre = jnp.dot(normed, w_dkv, preferred_element_type=jnp.float32)
    latent_power = lax.optimization_barrier(jnp.mean(latent_pre * latent_pre, axis=1, keepdims=True))
    latent_new = (latent_pre * lax.rsqrt(latent_power + epsilon) * latent_gain).astype(jnp.bfloat16)

    def one_session(inputs):
        absorbed_s, latent_s, owner_s, slot_s, cached_s = inputs
        cache = latent_pool[owner_s * POOL_DEV + slot_s].reshape(CACHE, LAT).astype(jnp.float32)
        queries = absorbed_s.astype(jnp.float32)
        latent_wide = latent_s.astype(jnp.float32)
        score_cache = jnp.einsum('tnl,cl->tnc', queries, cache, precision=exact_mode)
        score_new = jnp.einsum('tnl,jl->tnj', queries, latent_wide, precision=exact_mode)
        cache_ok = jnp.arange(CACHE, dtype=jnp.int32) < cached_s
        new_ok = jnp.arange(FRESH_SLOTS, dtype=jnp.int32)[None, :] <= jnp.arange(FRESH_SLOTS, dtype=jnp.int32)[:, None]
        score_cache = jnp.where(cache_ok[None, None, :], score_cache, -jnp.inf)
        score_new = jnp.where(new_ok[:, None, :], score_new, -jnp.inf)
        row_peak = jnp.maximum(lax.optimization_barrier(jnp.max(score_cache, axis=2, keepdims=True)), lax.optimization_barrier(jnp.max(score_new, axis=2, keepdims=True)))
        expo_cache = jnp.exp(score_cache - row_peak)
        expo_new = jnp.exp(score_new - row_peak)
        denominator = lax.optimization_barrier(jnp.sum(expo_cache, axis=2, keepdims=True)) + lax.optimization_barrier(jnp.sum(expo_new, axis=2, keepdims=True))
        probs_cache = (expo_cache / denominator).astype(jnp.bfloat16).astype(jnp.float32)
        probs_new = (expo_new / denominator).astype(jnp.bfloat16).astype(jnp.float32)
        attended = jnp.einsum('tnc,cl->tnl', probs_cache, cache, precision=exact_mode) + jnp.einsum('tnj,jl->tnl', probs_new, latent_wide, precision=exact_mode)
        return attended.astype(jnp.bfloat16)
    attended = lax.map(one_session, (absorbed.reshape(SESSION_COUNT, FRESH_SLOTS, HEADS, LAT), latent_new.reshape(SESSION_COUNT, FRESH_SLOTS, LAT), page_owner, page_slot, cached_len))
    mla = jnp.einsum('stnl,nlh->stnh', attended.astype(jnp.float32), w_uv.astype(jnp.float32), precision=exact_mode)
    mla_out = (mla * live[:, :, None, None]).reshape(TOKENS, HK).astype(jnp.bfloat16)
    return (resid_mid, final_state, mla_out)
```

```python
import functools
import math

import jax
import jax.numpy as jnp
from jax import lax
from jax.experimental import pallas as pl
from jax.experimental.pallas import tpu as pltpu
from jax.sharding import PartitionSpec as P

f32, bf16 = jnp.float32, jnp.bfloat16
EPS = 1e-6
CHUNK = 64
TILE = 128
BLOCKS = 2
MIB = 2**20


def mm(a, b, dims=((1,), (0,))):
    return lax.dot_general(
        a.astype(bf16), b.astype(bf16), (dims, ((), ())), preferred_element_type=f32
    )


def cost(flops, nbytes):
    return pl.CostEstimate(flops=int(flops), bytes_accessed=int(nbytes), transcendentals=0)


def whole(shape):
    return pl.BlockSpec(shape, lambda *_: (0,) * len(shape))


def delta_tokens(heads, first_row, new_len, q_ref, k_ref, v_ref, d_ref, b_ref, g_ref, gain, s_ref, store):
    rows = q_ref.shape[0]
    hd = s_ref.shape[-1]
    ri = lax.broadcasted_iota(jnp.int32, (TILE, TILE), 0)
    ci = lax.broadcasted_iota(jnp.int32, (TILE, TILE), 1)
    same = (ri // CHUNK) == (ci // CHUNK)
    lower = same & (ri >= ci)
    strict = same & (ri > ci)
    eye = (ri == ci).astype(f32)
    tri = lower.astype(bf16)
    levels = []
    b = 2
    while b <= CHUNK:
        half = b // 2
        levels.append(((ri // b) == (ci // b)) & ((ri // half) % 2 == 1) & ((ci // half) % 2 == 0))
        b *= 2
    tiles = rows // TILE
    work = [(t, h) for t in range(tiles) for h in range(heads)]
    row_id = lax.broadcasted_iota(jnp.int32, (TILE, hd), 0)
    lives = [(row_id + (first_row + t * TILE)) < new_len for t in range(tiles)]
    st = {}
    for t, h in work:
        rs = slice(t * TILE, (t + 1) * TILE)
        cs = slice(h * hd, (h + 1) * hd)
        live = lives[t]
        q = q_ref[rs, cs].astype(f32)
        k = k_ref[rs, cs].astype(f32)
        v = v_ref[rs, cs].astype(f32)
        dec = jnp.where(live, d_ref[rs, cs], 0.0)
        hi = dec.astype(bf16)
        lo = (dec - hi.astype(f32)).astype(bf16)
        cum = mm(tri, hi) + mm(tri, lo)
        beta = jnp.where(live, jnp.broadcast_to(b_ref[rs, h : h + 1], (TILE, hd)), 0.0)
        q = q * (lax.rsqrt(jnp.sum(q * q, axis=1, keepdims=True) + EPS) * (1.0 / math.sqrt(hd)))
        k = k * lax.rsqrt(jnp.sum(k * k, axis=1, keepdims=True) + EPS)
        grown = jnp.exp(cum)
        ke = k * grown
        qe = (q * grown).astype(bf16)
        kit = (k * jnp.exp(-cum)).T.astype(bf16)
        pair = mm(jnp.concatenate([ke.astype(bf16), qe], 0), kit)
        kk = jnp.where(strict, pair[:TILE], 0.0) * beta
        qk = jnp.where(lower, pair[TILE:], 0.0).astype(bf16)
        rhs = jnp.concatenate([(ke * beta).astype(bf16), (v * beta).astype(bf16)], 1)
        lasts = [
            jnp.broadcast_to(grown[(j + 1) * CHUNK - 1 : (j + 1) * CHUNK, :], (hd, hd)).T
            for j in range(TILE // CHUNK)
        ]
        st[t, h] = (kk, rhs, kit, qe, qk, lasts)
    invs = {w: eye - jnp.where(levels[0], st[w][0], 0.0) for w in work}
    for level in levels[1:]:
        left = {w: mm(invs[w], jnp.where(level, st[w][0], 0.0)) for w in work}
        invs = {w: invs[w] - mm(left[w], invs[w]) for w in work}
    solved = {w: mm(invs[w], st[w][1]) for w in work}
    state = [s_ref[h] for h in range(heads)]
    outs = {}
    for t in range(tiles):
        for j in range(TILE // CHUNK):
            r = slice(j * CHUNK, (j + 1) * CHUNK)
            seen = [
                mm(jnp.concatenate([solved[t, h][r, :hd].astype(bf16), st[t, h][3][r]], 0), state[h])
                for h in range(heads)
            ]
            for h in range(heads):
                _, _, kit, _, qk, lasts = st[t, h]
                fresh = solved[t, h][r, hd:] - seen[h][:CHUNK]
                outs[t, h, j] = seen[h][CHUNK:] + mm(qk[r, r], fresh)
                state[h] = lasts[j] * (state[h] + mm(kit[:, r], fresh))
    for h in range(heads):
        s_ref[h] = state[h]
    for t, h in work:
        rs = slice(t * TILE, (t + 1) * TILE)
        cs = slice(h * hd, (h + 1) * hd)
        o = jnp.concatenate([outs[t, h, j] for j in range(TILE // CHUNK)], 0)
        scale = lax.rsqrt(jnp.sum(o * o, axis=1, keepdims=True) * (1.0 / hd) + EPS)
        gate = 1.0 / (1.0 + jnp.exp(-g_ref[rs, cs].astype(f32)))
        store(rs, cs, jnp.where(lives[t], o * scale * gain * gate, 0.0).astype(bf16))


def delta_kernel(heads, block, head_devs, sc, q, k, v, d, b, g, gain, s0, resid, w_out,
                 s_ref, keep_ref, other_ref, mix_scr, ord_scr, res_scr, oth_scr):
    rows = q.shape[0]
    half, piece = rows // 2, rows // head_devs
    share = resid.shape[1]
    me = sc[1]
    chips = head_devs // 2
    core, chip = lax.rem(me, 2), lax.div(me, 2)
    s_ref[...] = s0[...]

    def store(rs, cs, value):
        mix_scr[rs, cs] = value

    delta_tokens(heads, block * rows, sc[0], q, k, v, d, b, g, gain[...], s_ref, store)
    for part in range(2):
        owner = (1 - core) if part == 0 else core
        for i in range(chips):
            at = pl.multiple_of(owner * half + lax.rem(chip + i, chips) * piece, piece)
            to = slice(part * half + i * piece, part * half + (i + 1) * piece)
            ord_scr[to, :] = mix_scr[pl.ds(at, piece), :]
            res_scr[to, :] = resid[pl.ds(at, piece), :]
    oth_scr[...] = jnp.dot(ord_scr[:half], w_out[...], preferred_element_type=f32)
    keep_ref[...] = jnp.dot(ord_scr[half:], w_out[...], preferred_element_type=f32)
    for dev in range(head_devs):
        @pl.when(me == dev)
        def _():
            cs = slice(dev * share, (dev + 1) * share)
            oth_scr[:, cs] += res_scr[:half].astype(f32)
            keep_ref[:, cs] += res_scr[half:].astype(f32)
    other_ref[...] = oth_scr[...].astype(bf16)


def delta_block(block, head_devs, scalars, q, k, v, dec, beta, gate, gain, state, resid, w_out):
    tokens, width = q.shape
    heads = beta.shape[1]
    hd = width // heads
    rows = tokens // BLOCKS
    share = resid.shape[1]
    full = w_out.shape[1]
    at = lambda i, s: (block, 0)
    spec = pl.BlockSpec((rows, width), at)
    return pl.pallas_call(
        functools.partial(delta_kernel, heads, block, head_devs),
        grid_spec=pltpu.PrefetchScalarGridSpec(
            num_scalar_prefetch=1,
            grid=(1,),
            in_specs=[spec, spec, spec, spec, pl.BlockSpec((rows, heads), at), spec, whole((1, hd)),
                      whole((heads, hd, hd)), pl.BlockSpec((rows, share), at), whole((width, full))],
            out_specs=[whole((heads, hd, hd)), whole((rows // 2, full)), whole((rows // 2, full))],
            scratch_shapes=[pltpu.VMEM((rows, width), bf16), pltpu.VMEM((rows, width), bf16),
                            pltpu.VMEM((rows, share), bf16), pltpu.VMEM((rows // 2, full), f32)],
        ),
        out_shape=[jax.ShapeDtypeStruct((heads, hd, hd), f32), jax.ShapeDtypeStruct((rows // 2, full), f32),
                   jax.ShapeDtypeStruct((rows // 2, full), bf16)],
        compiler_params=pltpu.CompilerParams(vmem_limit_bytes=40 * MIB),
        cost_estimate=cost(2 * rows * width * full * 3, 8 * MIB),
        name="delta",
    )(scalars, q, k, v, dec, beta, gate, gain, state, resid, w_out)


def pair_kernel(keep, got, own, *sends):
    piece = own.shape[0]
    for i in range(len(sends) + 1):
        r = slice(i * piece, (i + 1) * piece)
        total = keep[r, :] + got[r, :].astype(f32)
        if i == 0:
            own[...] = total
        else:
            sends[i - 1][...] = total.astype(bf16)


def pair_sum(keep, got, chips):
    rows, full = keep.shape
    piece = rows // chips
    return pl.pallas_call(
        pair_kernel,
        out_shape=[jax.ShapeDtypeStruct((piece, full), f32)]
        + [jax.ShapeDtypeStruct((piece, full), bf16)] * (chips - 1),
        compiler_params=pltpu.CompilerParams(vmem_limit_bytes=24 * MIB),
        cost_estimate=cost(rows * full, rows * full * 8),
        name="pair_sum",
    )(keep, got)


def sum_kernel(own, *refs):
    total = own[...]
    for ref in refs[:-1]:
        total = total + ref[...].astype(f32)
    refs[-1][...] = total.astype(bf16)


def sum_pieces(own, got):
    return pl.pallas_call(
        sum_kernel,
        out_shape=jax.ShapeDtypeStruct(own.shape, bf16),
        compiler_params=pltpu.CompilerParams(vmem_limit_bytes=24 * MIB),
        cost_estimate=cost(own.size * 4, own.size * 12),
        name="sum_pieces",
    )(own, *got)


def to_chip(x, step, devs):
    return lax.ppermute(x, "head", [(i, (i + 2 * step) % devs) for i in range(devs)])


def to_core(x, devs):
    return lax.ppermute(x, "head", [(i, i ^ 1) for i in range(devs)])


def share_all(x, devs):
    chips = devs // 2
    near = [(0, x)] + [((-s) % chips, to_chip(x, s, devs)) for s in range(1, chips)]
    far = [(step, to_core(a, devs)) for step, a in near]
    return [(0, step) for step, _ in near] + [(1, step) for step, _ in far], [a for _, a in near] + [a for _, a in far]


def latent_kernel(heads, block, order, page, sc, *refs):
    n = len(order)
    xs, refs = refs[:n], refs[n:]
    pages, refs = refs[:n], refs[n:]
    w_q, w_dkv, w_uk, w_uv, gain, latent_gain, refs = *refs[:6], refs[6:]
    olds, refs = refs[:block], refs[block:]
    resid_ref, out_ref, latent_ref, x_scr, n_scr = refs
    rows, full = x_scr.shape
    half, piece = rows // 2, rows // n
    share = resid_ref.shape[1]
    hd = w_uk.shape[1]
    new_len, me, cached_len = sc[0], sc[1], sc[2]
    core, chip = lax.rem(me, 2), lax.div(me, 2)
    chips = n // 2
    source = []
    for other, step in order:
        owner = (1 - core) if other else core
        source.append((owner, lax.rem(chip + step, chips)))
    for x, (owner, at) in zip(xs, source):
        x_scr[pl.ds(pl.multiple_of(owner * half + at * piece, piece), piece), :] = x[...]
    for dev in range(n):
        @pl.when(me == dev)
        def _():
            resid_ref[...] = x_scr[:, dev * share : (dev + 1) * share]
    wide = x_scr[...].astype(f32)
    power = jnp.sum(wide * wide, axis=1, keepdims=True) * (1.0 / full)
    n_scr[...] = (wide * lax.rsqrt(power + EPS) * gain[...]).astype(bf16)
    query = jnp.dot(n_scr[...], w_q[...], preferred_element_type=f32).astype(bf16)
    pre = jnp.dot(n_scr[...], w_dkv[...], preferred_element_type=f32)
    power = jnp.sum(pre * pre, axis=1, keepdims=True) * (1.0 / pre.shape[1])
    latent = (pre * lax.rsqrt(power + EPS) * latent_gain[...]).astype(bf16)
    latent_ref[...] = latent

    keys = [p[...] for p in pages] + [o[...] for o in olds] + [latent]
    count = pages[0].shape[0]
    per = page // n
    lane = lax.broadcasted_iota(jnp.int32, (1, count), 1)
    bias = []
    for owner, at in source:
        position = lax.div(lane, per) * page + (at * 2 + owner) * per + lax.rem(lane, per)
        bias.append(jnp.where(position < cached_len, 0.0, -jnp.inf))
    bias += [None] * block
    causal = lax.broadcasted_iota(jnp.int32, (rows, rows), 1) <= lax.broadcasted_iota(jnp.int32, (rows, rows), 0)
    live = (lax.broadcasted_iota(jnp.int32, (rows, hd), 0) + block * rows) < new_len
    for h in range(heads):
        absorbed = jnp.dot(query[:, h * hd : (h + 1) * hd], w_uk[h], preferred_element_type=f32)
        absorbed = (absorbed * (1.0 / math.sqrt(hd))).astype(bf16)
        scores = []
        for i, key in enumerate(keys):
            s = mm(absorbed, key, ((1,), (1,)))
            if i == len(keys) - 1:
                s = jnp.where(causal, s, -jnp.inf)
            elif bias[i] is not None:
                s = s + bias[i]
            scores.append(s)
        peak = jnp.max(scores[0], axis=1, keepdims=True)
        for s in scores[1:]:
            peak = jnp.maximum(peak, jnp.max(s, axis=1, keepdims=True))
        total, acc = 0.0, 0.0
        for s, key in zip(scores, keys):
            e = jnp.exp(s - peak)
            total = total + jnp.sum(e, axis=1, keepdims=True)
            acc = acc + mm(e, key)
        attended = (acc / total).astype(bf16)
        value = jnp.dot(attended, w_uv[h], preferred_element_type=f32)
        out_ref[:, h * hd : (h + 1) * hd] = jnp.where(live, value, 0.0).astype(bf16)


def latent_block(block, order, page, scalars, xs, pages, weights, olds):
    w_q, w_dkv, w_uk, w_uv, gain, latent_gain = weights
    heads, hd, lat = w_uk.shape
    rows, full = xs[0].shape[0] * len(xs), xs[0].shape[1]
    share = full // len(xs)
    args = [*xs, *pages, *weights, *olds]
    keys = pages[0].shape[0] * len(pages) + (block + 1) * rows
    flops = 2 * rows * (full * 2 * lat + heads * lat * (2 * hd + 2 * keys))
    return pl.pallas_call(
        functools.partial(latent_kernel, heads, block, order, page),
        grid_spec=pltpu.PrefetchScalarGridSpec(
            num_scalar_prefetch=1,
            grid=(1,),
            in_specs=[whole(a.shape) for a in args],
            out_specs=[whole((rows, share)), whole((rows, heads * hd)), whole((rows, lat))],
            scratch_shapes=[pltpu.VMEM((rows, full), bf16), pltpu.VMEM((rows, full), bf16)],
        ),
        out_shape=[jax.ShapeDtypeStruct((rows, share), bf16), jax.ShapeDtypeStruct((rows, heads * hd), bf16),
                   jax.ShapeDtypeStruct((rows, lat), bf16)],
        compiler_params=pltpu.CompilerParams(vmem_limit_bytes=50 * MIB),
        cost_estimate=cost(flops, 12 * MIB),
        name="latent",
    )(scalars, *args)


def fetch_rows(page_owner, page_slot, pool, me, devs):
    here = lax.axis_index("batch")
    owners = lax.axis_size("batch")
    page_count = page_owner.shape[1]
    most = max(2, 2 * page_count // owners)
    per = pool.shape[1] // devs
    hits = (page_owner == here).astype(jnp.int32)
    ranks = jnp.cumsum(hits, axis=1) - 1
    rank_ids = jnp.arange(most, dtype=jnp.int32)
    picked = hits[:, None, :] * (ranks[:, None, :] == rank_ids[None, :, None]).astype(jnp.int32)
    wanted = jnp.sum(picked * page_slot[:, None, :], axis=2)
    rows = lax.dynamic_slice_in_dim(pool, me * per, per, 1)
    outgoing = jnp.take(rows, wanted, axis=0, mode="clip")
    arrived = lax.all_to_all(outgoing, "batch", split_axis=0, concat_axis=0, tiled=True)
    flat = arrived.reshape((-1,) + arrived.shape[2:])
    mine = lax.dynamic_index_in_dim(page_owner, here, 0, keepdims=False)
    row = lax.broadcasted_iota(jnp.int32, (page_count, page_count), 0)
    col = lax.broadcasted_iota(jnp.int32, (page_count, page_count), 1)
    before = (mine[:, None] == mine[None, :]).astype(jnp.int32) * (col < row).astype(jnp.int32)
    place = mine * most + jnp.sum(before, axis=1)
    return jnp.take(flat, place, axis=0, mode="clip").reshape(page_count * per, pool.shape[2])


def on_device(
    resid_in, kda_q, kda_k, kda_v, log_decay, beta, out_gate, kda_gain, kda_state, w_out_kda, mla_gain,
    w_q, w_uk, w_dkv, latent_gain, latent_pool, page_owner, page_slot, cached_len, new_len, w_uv,
):
    devs = lax.axis_size("head")
    chips = devs // 2
    me = lax.axis_index("head")
    scalars = jnp.stack([new_len[0], me.astype(jnp.int32), cached_len[0]])

    my_rows = fetch_rows(page_owner, page_slot, latent_pool, me, devs)

    state = kda_state[0]
    gain = kda_gain.reshape(1, -1)
    owns = []
    for block in range(BLOCKS):
        state, keep, other = delta_block(
            block, devs, scalars, kda_q, kda_k, kda_v, log_decay, beta, out_gate, gain, state, resid_in, w_out_kda
        )
        own, *sends = pair_sum(keep, to_core(other, devs), chips)
        got = [to_chip(send, step + 1, devs) for step, send in enumerate(sends)]
        owns.append(sum_pieces(own, got))

    _, pages = share_all(my_rows, devs)
    weights = (w_q, w_dkv, w_uk, w_uv, mla_gain.reshape(1, -1), latent_gain.reshape(1, -1))
    resids, outs, latents = [], [], []
    for block in range(BLOCKS):
        order, xs = share_all(owns[block], devs)
        resid, out, latent = latent_block(
            block, order, latent_pool.shape[1], scalars, xs, pages, weights, latents
        )
        resids.append(resid)
        outs.append(out)
        latents.append(latent)
    return (jnp.concatenate(resids, 0), state[None], jnp.concatenate(outs, 0))


def solution(mesh):
    in_specs = (
        P("batch", "head"),
        P("batch", "head"),
        P("batch", "head"),
        P("batch", "head"),
        P("batch", "head"),
        P("batch", "head"),
        P("batch", "head"),
        P(),
        P("batch", "head", None, None),
        P("head", None),
        P(),
        P(None, "head"),
        P("head", None, None),
        P(),
        P(),
        P("batch", None, None),
        P(),
        P(),
        P("batch"),
        P("batch"),
        P("head", None, None),
    )
    out_specs = (P("batch", "head"), P("batch", "head", None, None), P("batch", "head"))
    return jax.shard_map(
        on_device, mesh=mesh, in_specs=in_specs, out_specs=out_specs, check_vma=False
    )
```

```python
import functools
import math

import jax
import jax.numpy as jnp
from jax import lax
from jax.experimental import pallas as pl
from jax.experimental.pallas import tpu as pltpu
from jax.sharding import PartitionSpec as P

f32, bf16 = jnp.float32, jnp.bfloat16
EPS = 1e-6
CHUNK = 64
TILE = 128
STEPS = 2
MIB = 2**20
DELTA_VMEM = 56 * MIB
LATENT_VMEM = 28 * MIB


def mm(a, b, dims=((1,), (0,))):
    return lax.dot_general(
        a.astype(bf16), b.astype(bf16), (dims, ((), ())), preferred_element_type=f32
    )


def cost(flops, nbytes):
    return pl.CostEstimate(flops=int(flops), bytes_accessed=int(nbytes), transcendentals=0)


def whole(shape):
    return pl.BlockSpec(shape, lambda *_: (0,) * len(shape))


def delta_tokens(heads, first_row, new_len, q_ref, k_ref, v_ref, d_ref, b_ref, g_ref, gain, s_ref, store):
    rows = q_ref.shape[0]
    hd = s_ref.shape[-1]
    ri = lax.broadcasted_iota(jnp.int32, (TILE, TILE), 0)
    ci = lax.broadcasted_iota(jnp.int32, (TILE, TILE), 1)
    same = (ri // CHUNK) == (ci // CHUNK)
    lower = same & (ri >= ci)
    strict = same & (ri > ci)
    eye = (ri == ci).astype(f32)
    tri = lower.astype(bf16)
    levels = []
    b = 2
    while b <= CHUNK:
        half = b // 2
        levels.append(((ri // b) == (ci // b)) & ((ri // half) % 2 == 1) & ((ci // half) % 2 == 0))
        b *= 2
    tiles = rows // TILE
    work = [(t, h) for t in range(tiles) for h in range(heads)]
    row_id = lax.broadcasted_iota(jnp.int32, (TILE, hd), 0)
    lives = [(row_id + (first_row + t * TILE)) < new_len for t in range(tiles)]
    st = {}
    for t, h in work:
        rs = slice(t * TILE, (t + 1) * TILE)
        cs = slice(h * hd, (h + 1) * hd)
        live = lives[t]
        q = q_ref[rs, cs].astype(f32)
        k = k_ref[rs, cs].astype(f32)
        v = v_ref[rs, cs].astype(f32)
        dec = jnp.where(live, d_ref[rs, cs], 0.0)
        hi = dec.astype(bf16)
        lo = (dec - hi.astype(f32)).astype(bf16)
        cum = mm(tri, hi) + mm(tri, lo)
        beta = jnp.where(live, jnp.broadcast_to(b_ref[h : h + 1, rs], (hd, TILE)).T, 0.0)
        q = q * (lax.rsqrt(jnp.sum(q * q, axis=1, keepdims=True) + EPS) * (1.0 / math.sqrt(hd)))
        k = k * lax.rsqrt(jnp.sum(k * k, axis=1, keepdims=True) + EPS)
        grown = jnp.exp(cum)
        ke = k * grown
        qe = (q * grown).astype(bf16)
        kit = (k * jnp.exp(-cum)).T.astype(bf16)
        pair = mm(jnp.concatenate([ke.astype(bf16), qe], 0), kit)
        kk = jnp.where(strict, pair[:TILE], 0.0) * beta
        qk = jnp.where(lower, pair[TILE:], 0.0).astype(bf16)
        rhs = jnp.concatenate([(ke * beta).astype(bf16), (v * beta).astype(bf16)], 1)
        lasts = [
            jnp.broadcast_to(grown[(j + 1) * CHUNK - 1 : (j + 1) * CHUNK, :], (hd, hd)).T
            for j in range(TILE // CHUNK)
        ]
        st[t, h] = (kk, rhs, kit, qe, qk, lasts)
    invs = {w: eye - jnp.where(levels[0], st[w][0], 0.0) for w in work}
    for level in levels[1:]:
        left = {w: mm(invs[w], jnp.where(level, st[w][0], 0.0)) for w in work}
        invs = {w: invs[w] - mm(left[w], invs[w]) for w in work}
    solved = {w: mm(invs[w], st[w][1]) for w in work}
    state = [s_ref[h] for h in range(heads)]
    outs = {}
    for t in range(tiles):
        for j in range(TILE // CHUNK):
            r = slice(j * CHUNK, (j + 1) * CHUNK)
            seen = [
                mm(jnp.concatenate([solved[t, h][r, :hd].astype(bf16), st[t, h][3][r]], 0), state[h])
                for h in range(heads)
            ]
            for h in range(heads):
                _, _, kit, _, qk, lasts = st[t, h]
                fresh = solved[t, h][r, hd:] - seen[h][:CHUNK]
                outs[t, h, j] = seen[h][CHUNK:] + mm(qk[r, r], fresh)
                state[h] = lasts[j] * (state[h] + mm(kit[:, r], fresh))
    for h in range(heads):
        s_ref[h] = state[h]
    for t, h in work:
        rs = slice(t * TILE, (t + 1) * TILE)
        cs = slice(h * hd, (h + 1) * hd)
        o = jnp.concatenate([outs[t, h, j] for j in range(TILE // CHUNK)], 0)
        scale = lax.rsqrt(jnp.sum(o * o, axis=1, keepdims=True) * (1.0 / hd) + EPS)
        gate = 1.0 / (1.0 + jnp.exp(-g_ref[rs, cs].astype(f32)))
        store(rs, cs, jnp.where(lives[t], o * scale * gain * gate, 0.0).astype(bf16))


def delta_kernel(heads, head_devs, sc, q, k, v, d, b, g, gain, s0, resid, w_hbm,
                 s_ref, keep_ref, other_ref, mix_scr, ord_scr, res_scr, oth_scr, w_scr, sem):
    step = pl.program_id(0)
    rows = q.shape[0]
    tokens = mix_scr.shape[0]
    half, piece = tokens // 2, tokens // head_devs
    share = resid.shape[0]
    me = sc[1]
    chips = head_devs // 2
    core, chip = lax.rem(me, 2), lax.div(me, 2)

    @pl.when(step == 0)
    def _():
        pltpu.make_async_copy(w_hbm, w_scr, sem).start()
        s_ref[...] = s0[...]

    def store(rs, cs, value):
        mix_scr[pl.ds(pl.multiple_of(step * rows + rs.start, TILE), TILE), cs] = value

    delta_tokens(heads, step * rows, sc[0], q, k, v, d, b, g, gain[...], s_ref, store)

    @pl.when(step == pl.num_programs(0) - 1)
    def _():
        for part in range(2):
            owner = (1 - core) if part == 0 else core
            for i in range(chips):
                at = pl.multiple_of(owner * half + lax.rem(chip + i, chips) * piece, piece)
                to = slice(part * half + i * piece, part * half + (i + 1) * piece)
                ord_scr[to, :] = mix_scr[pl.ds(at, piece), :]
        to = lax.broadcasted_iota(jnp.int32, (tokens, 1), 0)
        at = lax.broadcasted_iota(jnp.int32, (tokens, tokens), 1)
        owner = jnp.where(to < half, 1 - core, core)
        turn = lax.rem(chip + lax.div(lax.rem(to, half), piece), chips)
        order = (at == owner * half + turn * piece + lax.rem(to, piece)).astype(bf16)
        res_scr[...] = mm(order, resid[...], ((1,), (1,)))
        pltpu.make_async_copy(w_hbm, w_scr, sem).wait()
        oth_scr[...] = jnp.dot(ord_scr[:half], w_scr[...], preferred_element_type=f32)
        keep_ref[...] = jnp.dot(ord_scr[half:], w_scr[...], preferred_element_type=f32)
        for dev in range(head_devs):
            @pl.when(me == dev)
            def _():
                cs = slice(dev * share, (dev + 1) * share)
                oth_scr[:, cs] += res_scr[:half]
                keep_ref[:, cs] += res_scr[half:]
        other_ref[...] = oth_scr[...].astype(bf16)


def delta(head_devs, scalars, q, k, v, dec, beta, gate, gain, state, resid, w_out):
    tokens, width = q.shape
    heads = beta.shape[0]
    hd = width // heads
    rows = tokens // STEPS
    share = resid.shape[0]
    full = w_out.shape[1]
    spec = pl.BlockSpec((rows, width), lambda i, s: (i, 0))
    in_vmem = pl.BlockSpec(memory_space=pltpu.VMEM)
    return pl.pallas_call(
        functools.partial(delta_kernel, heads, head_devs),
        grid_spec=pltpu.PrefetchScalarGridSpec(
            num_scalar_prefetch=1,
            grid=(STEPS,),
            in_specs=[spec, spec, spec, spec, pl.BlockSpec((heads, rows), lambda i, s: (0, i)), spec, whole((1, hd)),
                      whole((heads, hd, hd)), whole((share, tokens)), pl.BlockSpec(memory_space=pl.ANY)],
            out_specs=[whole((heads, hd, hd)), in_vmem, in_vmem],
            scratch_shapes=[pltpu.VMEM((tokens, width), bf16), pltpu.VMEM((tokens, width), bf16),
                            pltpu.VMEM((tokens, share), f32), pltpu.VMEM((tokens // 2, full), f32),
                            pltpu.VMEM((width, full), bf16), pltpu.SemaphoreType.DMA],
        ),
        out_shape=[jax.ShapeDtypeStruct((heads, hd, hd), f32), jax.ShapeDtypeStruct((tokens // 2, full), f32),
                   jax.ShapeDtypeStruct((tokens // 2, full), bf16)],
        compiler_params=pltpu.CompilerParams(vmem_limit_bytes=DELTA_VMEM),
        cost_estimate=cost(2 * tokens * width * full * 3, 8 * MIB),
        name="delta",
    )(scalars, q, k, v, dec, beta, gate, gain, state, resid, w_out)


def pair_kernel(keep, got, own, *sends):
    piece = own.shape[0]
    for i in range(len(sends) + 1):
        r = slice(i * piece, (i + 1) * piece)
        total = keep[r, :] + got[r, :].astype(f32)
        if i == 0:
            own[...] = total
        else:
            sends[i - 1][...] = total.astype(bf16)


def pair_sum(keep, got, chips):
    rows, full = keep.shape
    piece = rows // chips
    return pl.pallas_call(
        pair_kernel,
        out_shape=[jax.ShapeDtypeStruct((piece, full), f32)]
        + [jax.ShapeDtypeStruct((piece, full), bf16)] * (chips - 1),
        compiler_params=pltpu.CompilerParams(vmem_limit_bytes=24 * MIB),
        cost_estimate=cost(rows * full, rows * full * 8),
        name="pair_sum",
    )(keep, got)


def sum_kernel(own, *refs):
    total = own[...]
    for ref in refs[:-1]:
        total = total + ref[...].astype(f32)
    refs[-1][...] = total.astype(bf16)


def sum_pieces(own, got):
    return pl.pallas_call(
        sum_kernel,
        out_shape=jax.ShapeDtypeStruct(own.shape, bf16),
        compiler_params=pltpu.CompilerParams(vmem_limit_bytes=24 * MIB),
        cost_estimate=cost(3e10, own.size * 12),
        name="sum_pieces",
    )(own, *got)


def to_chip(x, step, devs):
    return lax.ppermute(x, "head", [(i, (i + 2 * step) % devs) for i in range(devs)])


def to_core(x, devs):
    return lax.ppermute(x, "head", [(i, i ^ 1) for i in range(devs)])


def to_chips(x, devs):
    chips = devs // 2
    got = [to_chip(x, chips - step, devs) for step in range(1, chips)]
    return [x, *got]


def lanes(x, op):
    total = x[:, :128]
    for at in range(128, x.shape[1], 128):
        total = op(total, x[:, at : at + 128])
    return total


def sources(order, me):
    chips = len(order) // 2
    core, chip = lax.rem(me, 2), lax.div(me, 2)
    return [((1 - core) if other else core, lax.rem(chip + step, chips)) for other, step in order]


def validity(source, devs, page, count, cached_len):
    per = page // devs
    lane = lax.broadcasted_iota(jnp.int32, (1, count), 1)
    core, chip = source
    position = lax.div(lane, per) * page + (chip * 2 + core) * per + lax.rem(lane, per)
    return jnp.where(position < cached_len, 0.0, -jnp.inf)


def lay(keys, k_ref):
    at = 0
    for key in keys:
        k_ref[at : at + key.shape[0], :] = key[...]
        at += key.shape[0]


def attend(absorbed, widths, biases, state, k_ref, e_ref):
    scores, at = [], 0
    for width, bias in zip(widths, biases):
        scores.append(bias(mm(absorbed, k_ref[at : at + width, :], ((1,), (1,)))))
        at += width
    top = lanes(scores[0], jnp.maximum)
    for s in scores[1:]:
        top = jnp.maximum(top, lanes(s, jnp.maximum))
    top = jnp.max(top, axis=1, keepdims=True)
    peak = top if state is None else jnp.maximum(state[0], top)
    total, at = None, 0
    for s in scores:
        e = jnp.exp2(s - peak)
        add = lanes(e, jnp.add)
        total = add if total is None else total + add
        e_ref[:, at : at + s.shape[1]] = e.astype(bf16)
        at += s.shape[1]
    acc = jnp.dot(e_ref[:, :at], k_ref[:at, :], preferred_element_type=f32)
    if state is not None:
        shrink = jnp.exp2(state[0] - peak)
        total = total + state[1] * shrink
        acc = acc + state[2] * shrink
    return peak, total, acc


def load_kernel(*refs):
    count = len(refs) // 3
    copies = [pltpu.make_async_copy(refs[i], refs[count + i], refs[2 * count + i]) for i in range(count)]
    for copy in copies:
        copy.start()
    for copy in copies:
        copy.wait()


def load(*weights):
    return pl.pallas_call(
        load_kernel,
        in_specs=[pl.BlockSpec(memory_space=pl.ANY)] * len(weights),
        out_specs=[pl.BlockSpec(memory_space=pltpu.VMEM)] * len(weights),
        out_shape=[jax.ShapeDtypeStruct(w.shape, w.dtype) for w in weights],
        scratch_shapes=[pltpu.SemaphoreType.DMA] * len(weights),
        compiler_params=pltpu.CompilerParams(vmem_limit_bytes=8 * MIB),
        cost_estimate=cost(0, sum(w.size * 4 for w in weights)),
        name="load",
    )(*weights)


def front_kernel(heads, order, page, near, sc, *refs):
    n = len(order)
    xs, refs = refs[:n], refs[n:]
    pages, refs = refs[: len(near)], refs[len(near) :]
    w_q, w_dkv, w_uk, gain, latent_gain = refs[:5]
    resid_ref, absorbed_ref, peak_ref, total_ref, acc_ref = refs[5:10]
    x_scr, n_scr, r_scr, l_scr, k_scr, e_scr = refs[10:]
    rows, full = x_scr.shape
    half, piece = rows // 2, rows // n
    share = resid_ref.shape[0]
    hd = w_uk.shape[1]
    me, cached_len = sc[1], sc[2]
    source = sources(order, me)
    for x, (owner, at) in zip(xs, source):
        x_scr[pl.ds(pl.multiple_of(owner * half + at * piece, piece), piece), :] = x[...]
    for dev in range(n):
        @pl.when(me == dev)
        def _():
            r_scr[...] = x_scr[:, dev * share : (dev + 1) * share]
    eye = lax.broadcasted_iota(jnp.int32, (share, share), 0) == lax.broadcasted_iota(jnp.int32, (share, share), 1)
    resid_ref[...] = mm(eye, r_scr[...], ((1,), (1,))).astype(bf16)
    wide = x_scr[...].astype(f32)
    power = jnp.sum(wide * wide, axis=1, keepdims=True) * (1.0 / full)
    n_scr[...] = (wide * lax.rsqrt(power + EPS) * gain[...]).astype(bf16)
    query = jnp.dot(n_scr[...], w_q[...], preferred_element_type=f32).astype(bf16)
    pre = jnp.dot(n_scr[...], w_dkv[...], preferred_element_type=f32)
    power = jnp.sum(pre * pre, axis=1, keepdims=True) * (1.0 / pre.shape[1])
    l_scr[...] = (pre * lax.rsqrt(power + EPS) * latent_gain[...]).astype(bf16)
    count = pages[0].shape[0]
    valid = [validity(source[i], n, page, count, cached_len) for i in near]
    biases = [lambda s, v=v: s + v for v in valid]
    causal = lax.broadcasted_iota(jnp.int32, (rows, rows), 1) <= lax.broadcasted_iota(jnp.int32, (rows, rows), 0)
    biases.append(lambda s: jnp.where(causal, s, -jnp.inf))
    scale = math.log2(math.e) / math.sqrt(hd)
    keys = [*pages, l_scr]
    lay(keys, k_scr)
    widths = [key.shape[0] for key in keys]
    for h in range(heads):
        rs = slice(h * rows, (h + 1) * rows)
        absorbed = jnp.dot(query[:, h * hd : (h + 1) * hd], w_uk[h], preferred_element_type=f32) * scale
        absorbed_ref[rs, :] = absorbed.astype(bf16)
        peak, total, acc = attend(absorbed_ref[rs, :], widths, biases, None, k_scr, e_scr)
        peak_ref[rs, :] = jnp.broadcast_to(peak, total.shape)
        total_ref[rs, :] = total
        acc_ref[rs, :] = acc


def front(order, near, page, scalars, xs, pages, w_q, w_dkv, w_uk, gain, latent_gain):
    heads, hd, lat = w_uk.shape
    rows, full = xs[0].shape[0] * len(xs), xs[0].shape[1]
    share = full // len(xs)
    args = [*xs, *pages, w_q, w_dkv, w_uk, gain, latent_gain]
    keys = pages[0].shape[0] * len(near) + rows
    in_vmem = pl.BlockSpec(memory_space=pltpu.VMEM)
    return pl.pallas_call(
        functools.partial(front_kernel, heads, order, page, near),
        grid_spec=pltpu.PrefetchScalarGridSpec(
            num_scalar_prefetch=1,
            grid=(1,),
            in_specs=[in_vmem] * len(args),
            out_specs=[whole((share, rows))] + [in_vmem] * 4,
            scratch_shapes=[pltpu.VMEM((rows, full), bf16), pltpu.VMEM((rows, full), bf16),
                            pltpu.VMEM((rows, share), bf16), pltpu.VMEM((rows, lat), bf16),
                            pltpu.VMEM((keys, lat), bf16), pltpu.VMEM((rows, keys), bf16)],
        ),
        out_shape=[jax.ShapeDtypeStruct((share, rows), bf16), jax.ShapeDtypeStruct((heads * rows, lat), bf16),
                   jax.ShapeDtypeStruct((heads * rows, 128), f32), jax.ShapeDtypeStruct((heads * rows, 128), f32),
                   jax.ShapeDtypeStruct((heads * rows, lat), f32)],
        compiler_params=pltpu.CompilerParams(vmem_limit_bytes=LATENT_VMEM),
        cost_estimate=cost(2 * rows * (full * 2 * lat + heads * lat * (hd + 2 * keys)), 12 * MIB),
        name="front",
    )(scalars, *args)


def back_kernel(heads, order, page, far, sc, *refs):
    absorbed_ref, peak_ref, total_ref, acc_ref, refs = *refs[:4], refs[4:]
    pages, refs = refs[: len(far)], refs[len(far) :]
    w_uv, out_ref, k_scr, e_scr = refs
    rows = out_ref.shape[0]
    hd = w_uv.shape[2]
    new_len, me, cached_len = sc[0], sc[1], sc[2]
    source = sources(order, me)
    count = pages[0].shape[0]
    valid = [validity(source[i], len(order), page, count, cached_len) for i in far]
    biases = [lambda s, v=v: s + v for v in valid]
    live = lax.broadcasted_iota(jnp.int32, (rows, hd), 0) < new_len
    lay(pages, k_scr)
    widths = [count] * len(pages)
    for h in range(heads):
        rs = slice(h * rows, (h + 1) * rows)
        state = peak_ref[rs, 0:1], total_ref[rs, :], acc_ref[rs, :]
        _, total, acc = attend(absorbed_ref[rs, :], widths, biases, state, k_scr, e_scr)
        attended = (acc / jnp.sum(total, axis=1, keepdims=True)).astype(bf16)
        value = jnp.dot(attended, w_uv[h], preferred_element_type=f32)
        out_ref[:, h * hd : (h + 1) * hd] = jnp.where(live, value, 0.0).astype(bf16)


def back(order, far, page, scalars, state, pages, w_uv):
    heads, lat, hd = w_uv.shape
    rows = state[0].shape[0] // heads
    args = [*state, *pages, w_uv]
    keys = pages[0].shape[0] * len(far)
    return pl.pallas_call(
        functools.partial(back_kernel, heads, order, page, far),
        grid_spec=pltpu.PrefetchScalarGridSpec(
            num_scalar_prefetch=1,
            grid=(1,),
            in_specs=[pl.BlockSpec(memory_space=pltpu.VMEM)] * len(args),
            out_specs=whole((rows, heads * hd)),
            scratch_shapes=[pltpu.VMEM((keys, lat), bf16), pltpu.VMEM((rows, keys), bf16)],
        ),
        out_shape=jax.ShapeDtypeStruct((rows, heads * hd), bf16),
        compiler_params=pltpu.CompilerParams(vmem_limit_bytes=LATENT_VMEM),
        cost_estimate=cost(2 * rows * heads * lat * (hd + 2 * keys), 12 * MIB),
        name="back",
    )(scalars, *args)


def listed_rows(page_owner, page_slot, pool, me, devs):
    here = lax.axis_index("batch")
    owners = lax.axis_size("batch")
    page_count = page_owner.shape[1]
    most = max(2, 2 * page_count // owners)
    per = pool.shape[1] // devs
    before = jnp.arange(page_count, dtype=jnp.int32)
    earlier = before[None, :] < before[:, None]
    hits = page_owner == here
    ranks = jnp.sum((hits[:, None, :] & earlier[None]).astype(jnp.int32), axis=2)
    chosen = hits[:, None, :] & (ranks[:, None, :] == jnp.arange(most, dtype=jnp.int32)[None, :, None])
    wanted = jnp.sum(jnp.where(chosen, page_slot[:, None, :], 0), axis=2)
    rows = lax.dynamic_slice_in_dim(pool, me * per, per, 1)
    outgoing = jnp.take(rows, wanted, axis=0, mode="clip")
    mine = lax.dynamic_index_in_dim(page_owner, here, 0, keepdims=False)
    rank = jnp.sum(((mine[:, None] == mine[None, :]) & earlier).astype(jnp.int32), axis=1)
    return outgoing, mine * most + rank


def on_device(
    resid_in, kda_q, kda_k, kda_v, log_decay, beta, out_gate, kda_gain, kda_state, w_out_kda, mla_gain,
    w_q, w_uk, w_dkv, latent_gain, latent_pool, page_owner, page_slot, cached_len, new_len, w_uv,
):
    devs = lax.axis_size("head")
    chips = devs // 2
    me = lax.axis_index("head")
    scalars = jnp.stack([new_len[0], me.astype(jnp.int32), cached_len[0]])
    page = latent_pool.shape[1]

    state, keep, other = delta(
        devs, scalars, kda_q, kda_k, kda_v, log_decay, beta.T, out_gate, kda_gain.reshape(1, -1),
        kda_state[0], resid_in.T, w_out_kda
    )
    got = to_core(other, devs)
    outgoing, place = listed_rows(page_owner, page_slot, latent_pool, me, devs)
    own, *sends = pair_sum(keep, got, chips)
    sends, outgoing = lax.optimization_barrier((sends, outgoing))
    got = [to_chip(send, step + 1, devs) for step, send in enumerate(sends)]
    arrived = lax.all_to_all(outgoing, "batch", split_axis=0, concat_axis=0, tiled=True)
    flat = arrived.reshape((-1,) + arrived.shape[2:])

    x_here = to_chips(sum_pieces(own, got), devs)
    my_rows = jnp.take(flat, place, axis=0, mode="clip").reshape(-1, latent_pool.shape[2])
    pages_here = to_chips(my_rows, devs)
    near_page = to_core(my_rows, devs)
    w_q, w_dkv, near_page = lax.optimization_barrier((w_q, w_dkv, near_page))
    held_w = load(w_q, w_dkv)
    x_here[1:], near_page, held_w = lax.optimization_barrier((x_here[1:], near_page, held_w))
    xs = x_here + [to_core(x, devs) for x in x_here]
    order = [(0, step) for step in range(chips)] + [(1, step) for step in range(chips)]
    near, far = [0, chips], [i for i in range(devs) if i % chips]
    resid_mid, *held = front(
        order, near, page, scalars, xs, [my_rows, near_page], *held_w, w_uk, mla_gain.reshape(1, -1),
        latent_gain.reshape(1, -1)
    )
    others, resid_mid = lax.optimization_barrier((pages_here[1:], resid_mid))
    mla_out = back(order, far, page, scalars, held, others + [to_core(p, devs) for p in others], w_uv)
    return (resid_mid.T, state[None], mla_out)


def solution(mesh):
    in_specs = (
        P("batch", "head"),
        P("batch", "head"),
        P("batch", "head"),
        P("batch", "head"),
        P("batch", "head"),
        P("batch", "head"),
        P("batch", "head"),
        P(),
        P("batch", "head", None, None),
        P("head", None),
        P(),
        P(None, "head"),
        P("head", None, None),
        P(),
        P(),
        P("batch", None, None),
        P(),
        P(),
        P("batch"),
        P("batch"),
        P("head", None, None),
    )
    out_specs = (P("batch", "head"), P("batch", "head", None, None), P("batch", "head"))
    return jax.shard_map(
        on_device, mesh=mesh, in_specs=in_specs, out_specs=out_specs, check_vma=False
    )
```

```python
import functools
import math

import jax
import jax.numpy as jnp
from jax import lax
from jax.experimental import pallas as pl
from jax.experimental.pallas import tpu as pltpu
from jax.sharding import PartitionSpec as P

f32, bf16 = jnp.float32, jnp.bfloat16
EPS = 1e-6
CHUNK = 64
TILE = 128
STEPS = 2
MIB = 2**20
DELTA_VMEM = 56 * MIB
SUM_VMEM = 57 * MIB
LATENT_VMEM = 20 * MIB


def mm(a, b, dims=((1,), (0,))):
    return lax.dot_general(
        a.astype(bf16), b.astype(bf16), (dims, ((), ())), preferred_element_type=f32
    )


def cost(flops, nbytes):
    return pl.CostEstimate(flops=int(flops), bytes_accessed=int(nbytes), transcendentals=0)


def whole(shape):
    return pl.BlockSpec(shape, lambda *_: (0,) * len(shape))


def delta_tokens(heads, first_row, new_len, q_ref, k_ref, v_ref, d_ref, b_ref, g_ref, gain, s_ref, store):
    rows = q_ref.shape[0]
    hd = s_ref.shape[-1]
    ri = lax.broadcasted_iota(jnp.int32, (TILE, TILE), 0)
    ci = lax.broadcasted_iota(jnp.int32, (TILE, TILE), 1)
    same = (ri // CHUNK) == (ci // CHUNK)
    lower = same & (ri >= ci)
    strict = same & (ri > ci)
    eye = (ri == ci).astype(f32)
    tri = lower.astype(bf16)
    levels = []
    b = 2
    while b <= CHUNK:
        half = b // 2
        levels.append(((ri // b) == (ci // b)) & ((ri // half) % 2 == 1) & ((ci // half) % 2 == 0))
        b *= 2
    tiles = rows // TILE
    work = [(t, h) for t in range(tiles) for h in range(heads)]
    row_id = lax.broadcasted_iota(jnp.int32, (TILE, hd), 0)
    lives = [(row_id + (first_row + t * TILE)) < new_len for t in range(tiles)]
    st = {}
    for t, h in work:
        rs = slice(t * TILE, (t + 1) * TILE)
        cs = slice(h * hd, (h + 1) * hd)
        live = lives[t]
        q = q_ref[rs, cs].astype(f32)
        k = k_ref[rs, cs].astype(f32)
        v = v_ref[rs, cs].astype(f32)
        dec = jnp.where(live, d_ref[rs, cs], 0.0)
        hi = dec.astype(bf16)
        lo = (dec - hi.astype(f32)).astype(bf16)
        cum = mm(tri, hi) + mm(tri, lo)
        beta = jnp.where(live, jnp.broadcast_to(b_ref[h : h + 1, rs], (hd, TILE)).T, 0.0)
        q = q * (lax.rsqrt(jnp.sum(q * q, axis=1, keepdims=True) + EPS) * (1.0 / math.sqrt(hd)))
        k = k * lax.rsqrt(jnp.sum(k * k, axis=1, keepdims=True) + EPS)
        grown = jnp.exp(cum)
        ke = k * grown
        qe = (q * grown).astype(bf16)
        kit = (k * jnp.exp(-cum)).T.astype(bf16)
        pair = mm(jnp.concatenate([ke.astype(bf16), qe], 0), kit)
        kk = jnp.where(strict, pair[:TILE], 0.0) * beta
        qk = jnp.where(lower, pair[TILE:], 0.0).astype(bf16)
        rhs = jnp.concatenate([(ke * beta).astype(bf16), (v * beta).astype(bf16)], 1)
        lasts = [
            jnp.broadcast_to(grown[(j + 1) * CHUNK - 1 : (j + 1) * CHUNK, :], (hd, hd)).T
            for j in range(TILE // CHUNK)
        ]
        st[t, h] = (kk, rhs, kit, qe, qk, lasts)
    invs = {w: eye - jnp.where(levels[0], st[w][0], 0.0) for w in work}
    for level in levels[1:]:
        left = {w: mm(invs[w], jnp.where(level, st[w][0], 0.0)) for w in work}
        invs = {w: invs[w] - mm(left[w], invs[w]) for w in work}
    solved = {w: mm(invs[w], st[w][1]) for w in work}
    state = [s_ref[h] for h in range(heads)]
    outs = {}
    for t in range(tiles):
        for j in range(TILE // CHUNK):
            r = slice(j * CHUNK, (j + 1) * CHUNK)
            seen = [
                mm(jnp.concatenate([solved[t, h][r, :hd].astype(bf16), st[t, h][3][r]], 0), state[h])
                for h in range(heads)
            ]
            for h in range(heads):
                _, _, kit, _, qk, lasts = st[t, h]
                fresh = solved[t, h][r, hd:] - seen[h][:CHUNK]
                outs[t, h, j] = seen[h][CHUNK:] + mm(qk[r, r], fresh)
                state[h] = lasts[j] * (state[h] + mm(kit[:, r], fresh))
    for h in range(heads):
        s_ref[h] = state[h]
    for t, h in work:
        rs = slice(t * TILE, (t + 1) * TILE)
        cs = slice(h * hd, (h + 1) * hd)
        o = jnp.concatenate([outs[t, h, j] for j in range(TILE // CHUNK)], 0)
        scale = lax.rsqrt(jnp.sum(o * o, axis=1, keepdims=True) * (1.0 / hd) + EPS)
        gate = 1.0 / (1.0 + jnp.exp(-g_ref[rs, cs].astype(f32)))
        store(rs, cs, jnp.where(lives[t], o * scale * gain * gate, 0.0).astype(bf16))


def delta_kernel(heads, head_devs, sc, q, k, v, d, b, g, gain, s0, resid, w_hbm,
                 s_out, keep_ref, other_ref, s_ref, mix_scr, ord_scr, res_scr, sum_scr, out_scr, w_scr, sem, out_sem):
    step = pl.program_id(0)
    rows = q.shape[0]
    tokens = mix_scr.shape[0]
    half, piece = tokens // 2, tokens // head_devs
    share = resid.shape[0]
    me = sc[1]
    chips = head_devs // 2
    core, chip = lax.rem(me, 2), lax.div(me, 2)

    @pl.when(step == 0)
    def _():
        pltpu.make_async_copy(w_hbm, w_scr, sem).start()
        s_ref[...] = s0[...]

    def store(rs, cs, value):
        mix_scr[pl.ds(pl.multiple_of(step * rows + rs.start, TILE), TILE), cs] = value

    delta_tokens(heads, step * rows, sc[0], q, k, v, d, b, g, gain[...], s_ref, store)

    @pl.when(step == pl.num_programs(0) - 1)
    def _():
        for part in range(2):
            owner = (1 - core) if part == 0 else core
            for i in range(chips):
                at = pl.multiple_of(owner * half + lax.rem(chip + i, chips) * piece, piece)
                to = slice(part * half + i * piece, part * half + (i + 1) * piece)
                ord_scr[to, :] = mix_scr[pl.ds(at, piece), :]
        to = lax.broadcasted_iota(jnp.int32, (tokens, 1), 0)
        at = lax.broadcasted_iota(jnp.int32, (tokens, tokens), 1)
        owner = jnp.where(to < half, 1 - core, core)
        turn = lax.rem(chip + lax.div(lax.rem(to, half), piece), chips)
        order = (at == owner * half + turn * piece + lax.rem(to, piece)).astype(bf16)
        res_scr[...] = mm(order, resid[...], ((1,), (1,)))
        pltpu.make_async_copy(w_hbm, w_scr, sem).wait()
        copies = [pltpu.make_async_copy(s_ref, s_out, out_sem.at[2])]
        copies[0].start()
        for part, ref in enumerate((other_ref, keep_ref)):
            rs = slice(part * half, (part + 1) * half)
            sum_scr[...] = jnp.dot(ord_scr[rs], w_scr[...], preferred_element_type=f32)
            for dev in range(head_devs):
                @pl.when(me == dev)
                def _():
                    sum_scr[:, dev * share : (dev + 1) * share] += res_scr[rs]
            out_scr[part] = sum_scr[...].astype(bf16)
            copies.append(pltpu.make_async_copy(out_scr.at[part], ref, out_sem.at[part]))
            copies[-1].start()
        for copy in copies:
            copy.wait()


def delta(head_devs, scalars, q, k, v, dec, beta, gate, gain, state, resid, w_out):
    tokens, width = q.shape
    heads = beta.shape[0]
    hd = width // heads
    rows = tokens // STEPS
    share = resid.shape[0]
    full = w_out.shape[1]
    spec = pl.BlockSpec((rows, width), lambda i, s: (i, 0))
    in_hbm = pl.BlockSpec(memory_space=pl.ANY)
    return pl.pallas_call(
        functools.partial(delta_kernel, heads, head_devs),
        grid_spec=pltpu.PrefetchScalarGridSpec(
            num_scalar_prefetch=1,
            grid=(STEPS,),
            in_specs=[spec, spec, spec, spec, pl.BlockSpec((heads, rows), lambda i, s: (0, i)), spec, whole((1, hd)),
                      whole((heads, hd, hd)), whole((share, tokens)), in_hbm],
            out_specs=[in_hbm, in_hbm, in_hbm],
            scratch_shapes=[pltpu.VMEM((heads, hd, hd), f32), pltpu.VMEM((tokens, width), bf16),
                            pltpu.VMEM((tokens, width), bf16), pltpu.VMEM((tokens, share), f32), pltpu.VMEM((tokens // 2, full), f32),
                            pltpu.VMEM((2, tokens // 2, full), bf16), pltpu.VMEM((width, full), bf16),
                            pltpu.SemaphoreType.DMA, pltpu.SemaphoreType.DMA((3,))],
        ),
        out_shape=[jax.ShapeDtypeStruct((heads, hd, hd), f32), jax.ShapeDtypeStruct((tokens // 2, full), bf16),
                   jax.ShapeDtypeStruct((tokens // 2, full), bf16)],
        compiler_params=pltpu.CompilerParams(vmem_limit_bytes=DELTA_VMEM),
        cost_estimate=cost(2 * tokens * width * full * 3, 8 * MIB),
        name="delta",
    )(scalars, q, k, v, dec, beta, gate, gain, state, resid, w_out)


def pair_kernel(keep, got, own, *sends):
    piece = own.shape[0]
    for i in range(len(sends) + 1):
        r = slice(i * piece, (i + 1) * piece)
        total = keep[r, :].astype(f32) + got[r, :].astype(f32)
        if i == 0:
            own[...] = total
        else:
            sends[i - 1][...] = total.astype(bf16)


def pair_sum(keep, got, chips):
    rows, full = keep.shape
    piece = rows // chips
    return pl.pallas_call(
        pair_kernel,
        in_specs=[pl.BlockSpec(memory_space=pltpu.VMEM)] * 2,
        out_specs=[pl.BlockSpec(memory_space=pltpu.VMEM)] * chips,
        out_shape=[jax.ShapeDtypeStruct((piece, full), f32)]
        + [jax.ShapeDtypeStruct((piece, full), bf16)] * (chips - 1),
        compiler_params=pltpu.CompilerParams(vmem_limit_bytes=10 * MIB),
        cost_estimate=cost(rows * full, rows * full * 8),
        name="pair_sum",
    )(keep, got)


def pace_kernel(place, total, out):
    out[...] = place[...]


def pace(place, total):
    return pl.pallas_call(
        pace_kernel,
        in_specs=[pl.BlockSpec(memory_space=pltpu.VMEM), pl.BlockSpec(memory_space=pl.ANY)],
        out_specs=pl.BlockSpec(memory_space=pltpu.VMEM),
        out_shape=jax.ShapeDtypeStruct(place.shape, place.dtype),
        compiler_params=pltpu.CompilerParams(vmem_limit_bytes=2 * MIB),
        cost_estimate=cost(1.2e10, 0),
        name="pace",
    )(place, total)


def to_chip(x, step, devs):
    return lax.ppermute(x, "head", [(i, (i + 2 * step) % devs) for i in range(devs)])


def to_core(x, devs):
    return lax.ppermute(x, "head", [(i, i ^ 1) for i in range(devs)])


def to_chips(x, devs):
    chips = devs // 2
    got = [to_chip(x, chips - step, devs) for step in range(1, chips)]
    return [x, *got]


def lanes(x, op):
    total = x[:, :128]
    for at in range(128, x.shape[1], 128):
        total = op(total, x[:, at : at + 128])
    return total


def sources(order, me):
    chips = len(order) // 2
    core, chip = lax.rem(me, 2), lax.div(me, 2)
    return [((1 - core) if other else core, lax.rem(chip + step, chips)) for other, step in order]


def validity(source, devs, page, count, cached_len):
    per = page // devs
    lane = lax.broadcasted_iota(jnp.int32, (1, count), 1)
    core, chip = source
    position = lax.div(lane, per) * page + (chip * 2 + core) * per + lax.rem(lane, per)
    return jnp.where(position < cached_len, 0.0, -jnp.inf)


def lay(keys, k_ref):
    at = 0
    for key in keys:
        k_ref[at : at + key.shape[0], :] = key[...]
        at += key.shape[0]


def score(absorbed, widths, biases, k_ref):
    scores, top, at = [], None, 0
    for width, bias in zip(widths, biases):
        s = bias(mm(absorbed, k_ref[at : at + width, :], ((1,), (1,))))
        scores.append(s)
        best = lanes(s, jnp.maximum)
        top = best if top is None else jnp.maximum(top, best)
        at += width
    return scores, top


def attend(scored, state, k_ref, e_ref):
    scores, top = scored
    top = jnp.max(top, axis=1, keepdims=True)
    peak = top if state is None else jnp.maximum(state[0], top)
    total, at = None, 0
    for s in scores:
        e = jnp.exp2(s - peak)
        add = lanes(e, jnp.add)
        total = add if total is None else total + add
        e_ref[:, at : at + s.shape[1]] = e.astype(bf16)
        at += s.shape[1]
    acc = jnp.dot(e_ref[:, :at], k_ref[:at, :], preferred_element_type=f32)
    if state is not None:
        shrink = jnp.exp2(state[0] - peak)
        total = total + state[1] * shrink
        acc = acc + state[2] * shrink
    return peak, total, acc


def load_kernel(*refs):
    count = len(refs) // 3
    copies = [pltpu.make_async_copy(refs[i], refs[count + i], refs[2 * count + i]) for i in range(count)]
    for copy in copies:
        copy.start()
    for copy in copies:
        copy.wait()


def load(*weights):
    return pl.pallas_call(
        load_kernel,
        in_specs=[pl.BlockSpec(memory_space=pl.ANY)] * len(weights),
        out_specs=[pl.BlockSpec(memory_space=pltpu.VMEM)] * len(weights),
        out_shape=[jax.ShapeDtypeStruct(w.shape, w.dtype) for w in weights],
        scratch_shapes=[pltpu.SemaphoreType.DMA] * len(weights),
        compiler_params=pltpu.CompilerParams(vmem_limit_bytes=8 * MIB),
        cost_estimate=cost(0, sum(w.size * 4 for w in weights)),
        name="load",
    )(*weights)


def front_kernel(heads, order, page, near, sc, *refs):
    n = len(order)
    xs, refs = refs[:n], refs[n:]
    pages, refs = refs[: len(near)], refs[len(near) :]
    w_q, w_dkv, w_uk, gain, latent_gain = refs[:5]
    resid_ref, absorbed_ref, peak_ref, total_ref, acc_ref = refs[5:10]
    x_scr, n_scr, r_scr, l_scr, k_scr, e_scr = refs[10:]
    rows, full = x_scr.shape
    half, piece = rows // 2, rows // n
    share = resid_ref.shape[0]
    hd = w_uk.shape[1]
    me, cached_len = sc[1], sc[2]
    source = sources(order, me)
    for x, (owner, at) in zip(xs, source):
        x_scr[pl.ds(pl.multiple_of(owner * half + at * piece, piece), piece), :] = x[...]
    for dev in range(n):
        @pl.when(me == dev)
        def _():
            r_scr[...] = x_scr[:, dev * share : (dev + 1) * share]
    eye = lax.broadcasted_iota(jnp.int32, (share, share), 0) == lax.broadcasted_iota(jnp.int32, (share, share), 1)
    resid_ref[...] = mm(eye, r_scr[...], ((1,), (1,))).astype(bf16)
    wide = x_scr[...].astype(f32)
    power = jnp.sum(wide * wide, axis=1, keepdims=True) * (1.0 / full)
    n_scr[...] = (wide * lax.rsqrt(power + EPS) * gain[...]).astype(bf16)
    query = jnp.dot(n_scr[...], w_q[...], preferred_element_type=f32).astype(bf16)
    pre = jnp.dot(n_scr[...], w_dkv[...], preferred_element_type=f32)
    power = jnp.sum(pre * pre, axis=1, keepdims=True) * (1.0 / pre.shape[1])
    l_scr[...] = (pre * lax.rsqrt(power + EPS) * latent_gain[...]).astype(bf16)
    count = pages[0].shape[0]
    valid = [validity(source[i], n, page, count, cached_len) for i in near]
    biases = [lambda s, v=v: s + v for v in valid]
    causal = lax.broadcasted_iota(jnp.int32, (rows, rows), 1) <= lax.broadcasted_iota(jnp.int32, (rows, rows), 0)
    biases.append(lambda s: jnp.where(causal, s, -jnp.inf))
    scale = math.log2(math.e) / math.sqrt(hd)
    keys = [*pages, l_scr]
    lay(keys, k_scr)
    widths = [key.shape[0] for key in keys]

    def scores_of(h):
        rs = slice(h * rows, (h + 1) * rows)
        absorbed = jnp.dot(query[:, h * hd : (h + 1) * hd], w_uk[h], preferred_element_type=f32) * scale
        absorbed_ref[rs, :] = absorbed.astype(bf16)
        return score(absorbed_ref[rs, :], widths, biases, k_scr)

    scored = scores_of(0)
    for h in range(heads):
        rs = slice(h * rows, (h + 1) * rows)
        later = scores_of(h + 1) if h + 1 < heads else None
        peak, total, acc = attend(scored, None, k_scr, e_scr.at[h % 2])
        scored = later
        peak_ref[rs, :] = jnp.broadcast_to(peak, total.shape)
        total_ref[rs, :] = total
        acc_ref[rs, :] = acc


def front(order, near, page, scalars, xs, pages, w_q, w_dkv, w_uk, gain, latent_gain):
    heads, hd, lat = w_uk.shape
    rows, full = xs[0].shape[0] * len(xs), xs[0].shape[1]
    share = full // len(xs)
    args = [*xs, *pages, w_q, w_dkv, w_uk, gain, latent_gain]
    keys = pages[0].shape[0] * len(near) + rows
    in_vmem = pl.BlockSpec(memory_space=pltpu.VMEM)
    return pl.pallas_call(
        functools.partial(front_kernel, heads, order, page, near),
        grid_spec=pltpu.PrefetchScalarGridSpec(
            num_scalar_prefetch=1,
            grid=(1,),
            in_specs=[in_vmem] * len(args),
            out_specs=[whole((share, rows))] + [in_vmem] * 4,
            scratch_shapes=[pltpu.VMEM((rows, full), bf16), pltpu.VMEM((rows, full), bf16),
                            pltpu.VMEM((rows, share), bf16), pltpu.VMEM((rows, lat), bf16),
                            pltpu.VMEM((keys, lat), bf16), pltpu.VMEM((2, rows, keys), bf16)],
        ),
        out_shape=[jax.ShapeDtypeStruct((share, rows), bf16), jax.ShapeDtypeStruct((heads * rows, lat), bf16),
                   jax.ShapeDtypeStruct((heads * rows, 128), f32), jax.ShapeDtypeStruct((heads * rows, 128), f32),
                   jax.ShapeDtypeStruct((heads * rows, lat), f32)],
        compiler_params=pltpu.CompilerParams(vmem_limit_bytes=LATENT_VMEM),
        cost_estimate=cost(2 * rows * (full * 2 * lat + heads * lat * (hd + 2 * keys)), 12 * MIB),
        name="front",
    )(scalars, *args)


def back_kernel(heads, order, page, far, sc, *refs):
    absorbed_ref, peak_ref, total_ref, acc_ref, refs = *refs[:4], refs[4:]
    pages, refs = refs[: len(far)], refs[len(far) :]
    w_uv, out_ref, k_scr, e_scr = refs
    rows = out_ref.shape[0]
    hd = w_uv.shape[2]
    new_len, me, cached_len = sc[0], sc[1], sc[2]
    source = sources(order, me)
    count = pages[0].shape[0]
    valid = [validity(source[i], len(order), page, count, cached_len) for i in far]
    biases = [lambda s, v=v: s + v for v in valid]
    live = lax.broadcasted_iota(jnp.int32, (rows, hd), 0) < new_len
    lay(pages, k_scr)
    widths = [count] * len(pages)
    scored = score(absorbed_ref[:rows, :], widths, biases, k_scr)
    for h in range(heads):
        rs = slice(h * rows, (h + 1) * rows)
        later = score(absorbed_ref[(h + 1) * rows : (h + 2) * rows, :], widths, biases, k_scr) if h + 1 < heads else None
        state = peak_ref[rs, 0:1], total_ref[rs, :], acc_ref[rs, :]
        _, total, acc = attend(scored, state, k_scr, e_scr.at[h % 2])
        scored = later
        attended = (acc / jnp.sum(total, axis=1, keepdims=True)).astype(bf16)
        value = jnp.dot(attended, w_uv[h], preferred_element_type=f32)
        out_ref[:, h * hd : (h + 1) * hd] = jnp.where(live, value, 0.0).astype(bf16)


def back(order, far, page, scalars, state, pages, w_uv):
    heads, lat, hd = w_uv.shape
    rows = state[0].shape[0] // heads
    args = [*state, *pages, w_uv]
    keys = pages[0].shape[0] * len(far)
    return pl.pallas_call(
        functools.partial(back_kernel, heads, order, page, far),
        grid_spec=pltpu.PrefetchScalarGridSpec(
            num_scalar_prefetch=1,
            grid=(1,),
            in_specs=[pl.BlockSpec(memory_space=pltpu.VMEM)] * len(args),
            out_specs=whole((rows, heads * hd)),
            scratch_shapes=[pltpu.VMEM((keys, lat), bf16), pltpu.VMEM((2, rows, keys), bf16)],
        ),
        out_shape=jax.ShapeDtypeStruct((rows, heads * hd), bf16),
        compiler_params=pltpu.CompilerParams(vmem_limit_bytes=LATENT_VMEM),
        cost_estimate=cost(2 * rows * heads * lat * (hd + 2 * keys), 12 * MIB),
        name="back",
    )(scalars, *args)


def listed_rows(page_owner, page_slot, pool, me, devs):
    here = lax.axis_index("batch")
    owners = lax.axis_size("batch")
    page_count = page_owner.shape[1]
    most = max(2, 2 * page_count // owners)
    per = pool.shape[1] // devs
    before = jnp.arange(page_count, dtype=jnp.int32)
    earlier = before[None, :] < before[:, None]
    hits = page_owner == here
    ranks = jnp.sum((hits[:, None, :] & earlier[None]).astype(jnp.int32), axis=2)
    chosen = hits[:, None, :] & (ranks[:, None, :] == jnp.arange(most, dtype=jnp.int32)[None, :, None])
    wanted = jnp.sum(jnp.where(chosen, page_slot[:, None, :], 0), axis=2)
    rows = lax.dynamic_slice_in_dim(pool, me * per, per, 1)
    outgoing = jnp.take(rows, wanted, axis=0, mode="clip")
    mine = lax.dynamic_index_in_dim(page_owner, here, 0, keepdims=False)
    rank = jnp.sum(((mine[:, None] == mine[None, :]) & earlier).astype(jnp.int32), axis=1)
    return outgoing, mine * most + rank


def on_device(
    resid_in, kda_q, kda_k, kda_v, log_decay, beta, out_gate, kda_gain, kda_state, w_out_kda, mla_gain,
    w_q, w_uk, w_dkv, latent_gain, latent_pool, page_owner, page_slot, cached_len, new_len, w_uv,
):
    devs = lax.axis_size("head")
    chips = devs // 2
    me = lax.axis_index("head")
    scalars = jnp.stack([new_len[0], me.astype(jnp.int32), cached_len[0]])
    page = latent_pool.shape[1]

    state, keep, other = delta(
        devs, scalars, kda_q, kda_k, kda_v, log_decay, beta.T, out_gate, kda_gain.reshape(1, -1),
        kda_state[0], resid_in.T, w_out_kda
    )
    got = to_core(other, devs)
    outgoing, place = listed_rows(page_owner, page_slot, latent_pool, me, devs)
    own, *sends = pair_sum(keep, got, chips)
    sends, outgoing = lax.optimization_barrier((sends, outgoing))
    got = [to_chip(send, step + 1, devs) for step, send in enumerate(sends)]
    arrived = lax.all_to_all(outgoing, "batch", split_axis=0, concat_axis=0, tiled=True)
    flat = arrived.reshape((-1,) + arrived.shape[2:])

    total = own
    for part in got:
        total = total + part.astype(f32)
    total = total.astype(bf16)
    x_here = to_chips(total, devs)
    place = pace(place, total)
    my_rows = jnp.take(flat, place, axis=0, mode="clip").reshape(-1, latent_pool.shape[2])
    pages_here = to_chips(my_rows, devs)
    near_page = to_core(my_rows, devs)
    w_q, w_dkv, near_page = lax.optimization_barrier((w_q, w_dkv, near_page))
    held_w = load(w_q, w_dkv)
    x_here[1:], near_page, held_w = lax.optimization_barrier((x_here[1:], near_page, held_w))
    xs = x_here + [to_core(x, devs) for x in x_here]
    order = [(0, step) for step in range(chips)] + [(1, step) for step in range(chips)]
    near, far = [0, chips], [i for i in range(devs) if i % chips]
    resid_mid, *held = front(
        order, near, page, scalars, xs, [my_rows, near_page], *held_w, w_uk, mla_gain.reshape(1, -1),
        latent_gain.reshape(1, -1)
    )
    others, resid_mid = lax.optimization_barrier((pages_here[1:], resid_mid))
    mla_out = back(order, far, page, scalars, held, others + [to_core(p, devs) for p in others], w_uv)
    return (resid_mid.T, state[None], mla_out)


def solution(mesh):
    in_specs = (
        P("batch", "head"),
        P("batch", "head"),
        P("batch", "head"),
        P("batch", "head"),
        P("batch", "head"),
        P("batch", "head"),
        P("batch", "head"),
        P(),
        P("batch", "head", None, None),
        P("head", None),
        P(),
        P(None, "head"),
        P("head", None, None),
        P(),
        P(),
        P("batch", None, None),
        P(),
        P(),
        P("batch"),
        P("batch"),
        P("head", None, None),
    )
    out_specs = (P("batch", "head"), P("batch", "head", None, None), P("batch", "head"))
    return jax.shard_map(
        on_device, mesh=mesh, in_specs=in_specs, out_specs=out_specs, check_vma=False
    )
```

```python
import functools
import math

import jax
import jax.numpy as jnp
from jax import lax
from jax.experimental import pallas as pl
from jax.experimental.pallas import tpu as pltpu
from jax.sharding import PartitionSpec as P

f32, bf16 = jnp.float32, jnp.bfloat16
EPS = 1e-6
CHUNK = 64
TILE = 128
STEPS = 2
MIB = 2**20
DELTA_VMEM = 56 * MIB
FRONT_VMEM = 43 * MIB
LATENT_VMEM = 20 * MIB


def mm(a, b, dims=((1,), (0,))):
    return lax.dot_general(
        a.astype(bf16), b.astype(bf16), (dims, ((), ())), preferred_element_type=f32
    )


def cost(flops, nbytes):
    return pl.CostEstimate(flops=int(flops), bytes_accessed=int(nbytes), transcendentals=0)


def whole(shape):
    return pl.BlockSpec(shape, lambda *_: (0,) * len(shape))


def delta_tokens(heads, first_row, new_len, q_ref, k_ref, v_ref, d_ref, b_ref, g_ref, gain, s_ref, store):
    rows = q_ref.shape[0]
    hd = s_ref.shape[-1]
    ri = lax.broadcasted_iota(jnp.int32, (TILE, TILE), 0)
    ci = lax.broadcasted_iota(jnp.int32, (TILE, TILE), 1)
    same = (ri // CHUNK) == (ci // CHUNK)
    lower = same & (ri >= ci)
    strict = same & (ri > ci)
    eye = (ri == ci).astype(f32)
    tri = lower.astype(bf16)
    levels = []
    b = 2
    while b <= CHUNK:
        half = b // 2
        levels.append(((ri // b) == (ci // b)) & ((ri // half) % 2 == 1) & ((ci // half) % 2 == 0))
        b *= 2
    tiles = rows // TILE
    work = [(t, h) for t in range(tiles) for h in range(heads)]
    row_id = lax.broadcasted_iota(jnp.int32, (TILE, hd), 0)
    lives = [(row_id + (first_row + t * TILE)) < new_len for t in range(tiles)]
    st = {}
    for t, h in work:
        rs = slice(t * TILE, (t + 1) * TILE)
        cs = slice(h * hd, (h + 1) * hd)
        live = lives[t]
        q = q_ref[rs, cs].astype(f32)
        k = k_ref[rs, cs].astype(f32)
        v = v_ref[rs, cs].astype(f32)
        dec = jnp.where(live, d_ref[rs, cs], 0.0)
        hi = dec.astype(bf16)
        lo = (dec - hi.astype(f32)).astype(bf16)
        cum = mm(tri, hi) + mm(tri, lo)
        beta = jnp.where(live, jnp.broadcast_to(b_ref[h : h + 1, rs], (hd, TILE)).T, 0.0)
        q = q * (lax.rsqrt(jnp.sum(q * q, axis=1, keepdims=True) + EPS) * (1.0 / math.sqrt(hd)))
        k = k * lax.rsqrt(jnp.sum(k * k, axis=1, keepdims=True) + EPS)
        grown = jnp.exp(cum)
        ke = k * grown
        qe = (q * grown).astype(bf16)
        kit = (k * jnp.exp(-cum)).T.astype(bf16)
        pair = mm(jnp.concatenate([ke.astype(bf16), qe], 0), kit)
        kk = jnp.where(strict, pair[:TILE], 0.0) * beta
        qk = jnp.where(lower, pair[TILE:], 0.0).astype(bf16)
        rhs = jnp.concatenate([(ke * beta).astype(bf16), (v * beta).astype(bf16)], 1)
        lasts = [
            jnp.broadcast_to(grown[(j + 1) * CHUNK - 1 : (j + 1) * CHUNK, :], (hd, hd)).T
            for j in range(TILE // CHUNK)
        ]
        st[t, h] = (kk, rhs, kit, qe, qk, lasts)
    invs = {w: eye - jnp.where(levels[0], st[w][0], 0.0) for w in work}
    for level in levels[1:]:
        left = {w: mm(invs[w], jnp.where(level, st[w][0], 0.0)) for w in work}
        invs = {w: invs[w] - mm(left[w], invs[w]) for w in work}
    solved = {w: mm(invs[w], st[w][1]) for w in work}
    state = [s_ref[h] for h in range(heads)]
    outs = {}
    for t in range(tiles):
        for j in range(TILE // CHUNK):
            r = slice(j * CHUNK, (j + 1) * CHUNK)
            seen = [
                mm(jnp.concatenate([solved[t, h][r, :hd].astype(bf16), st[t, h][3][r]], 0), state[h])
                for h in range(heads)
            ]
            for h in range(heads):
                _, _, kit, _, qk, lasts = st[t, h]
                fresh = solved[t, h][r, hd:] - seen[h][:CHUNK]
                outs[t, h, j] = seen[h][CHUNK:] + mm(qk[r, r], fresh)
                state[h] = lasts[j] * (state[h] + mm(kit[:, r], fresh))
    for h in range(heads):
        s_ref[h] = state[h]
    for t, h in work:
        rs = slice(t * TILE, (t + 1) * TILE)
        cs = slice(h * hd, (h + 1) * hd)
        o = jnp.concatenate([outs[t, h, j] for j in range(TILE // CHUNK)], 0)
        scale = lax.rsqrt(jnp.sum(o * o, axis=1, keepdims=True) * (1.0 / hd) + EPS)
        gate = 1.0 / (1.0 + jnp.exp(-g_ref[rs, cs].astype(f32)))
        store(rs, cs, jnp.where(lives[t], o * scale * gain * gate, 0.0).astype(bf16))


def delta_kernel(heads, head_devs, sc, q, k, v, d, b, g, gain, s0, resid, w_hbm,
                 s_out, keep_ref, other_ref, s_ref, mix_scr, ord_scr, res_scr, sum_scr, out_scr, w_scr, sem, out_sem):
    step = pl.program_id(0)
    rows = q.shape[0]
    tokens = mix_scr.shape[0]
    half, piece = tokens // 2, tokens // head_devs
    share = resid.shape[0]
    me = sc[1]
    chips = head_devs // 2
    core, chip = lax.rem(me, 2), lax.div(me, 2)

    @pl.when(step == 0)
    def _():
        pltpu.make_async_copy(w_hbm, w_scr, sem).start()
        s_ref[...] = s0[...]

    def store(rs, cs, value):
        mix_scr[pl.ds(pl.multiple_of(step * rows + rs.start, TILE), TILE), cs] = value

    delta_tokens(heads, step * rows, sc[0], q, k, v, d, b, g, gain[...], s_ref, store)

    @pl.when(step == pl.num_programs(0) - 1)
    def _():
        for part in range(2):
            owner = (1 - core) if part == 0 else core
            for i in range(chips):
                at = pl.multiple_of(owner * half + lax.rem(chip + i, chips) * piece, piece)
                to = slice(part * half + i * piece, part * half + (i + 1) * piece)
                ord_scr[to, :] = mix_scr[pl.ds(at, piece), :]
        to = lax.broadcasted_iota(jnp.int32, (tokens, 1), 0)
        at = lax.broadcasted_iota(jnp.int32, (tokens, tokens), 1)
        owner = jnp.where(to < half, 1 - core, core)
        turn = lax.rem(chip + lax.div(lax.rem(to, half), piece), chips)
        order = (at == owner * half + turn * piece + lax.rem(to, piece)).astype(bf16)
        res_scr[...] = mm(order, resid[...], ((1,), (1,)))
        pltpu.make_async_copy(w_hbm, w_scr, sem).wait()
        copies = [pltpu.make_async_copy(s_ref, s_out, out_sem.at[2])]
        copies[0].start()
        for part, ref in enumerate((other_ref, keep_ref)):
            rs = slice(part * half, (part + 1) * half)
            sum_scr[...] = jnp.dot(ord_scr[rs], w_scr[...], preferred_element_type=f32)
            for dev in range(head_devs):
                @pl.when(me == dev)
                def _():
                    sum_scr[:, dev * share : (dev + 1) * share] += res_scr[rs]
            out_scr[part] = sum_scr[...].astype(bf16)
            copies.append(pltpu.make_async_copy(out_scr.at[part], ref, out_sem.at[part]))
            copies[-1].start()
        for copy in copies:
            copy.wait()


def delta(head_devs, scalars, q, k, v, dec, beta, gate, gain, state, resid, w_out):
    tokens, width = q.shape
    heads = beta.shape[0]
    hd = width // heads
    rows = tokens // STEPS
    share = resid.shape[0]
    full = w_out.shape[1]
    spec = pl.BlockSpec((rows, width), lambda i, s: (i, 0))
    in_hbm = pl.BlockSpec(memory_space=pl.ANY)
    return pl.pallas_call(
        functools.partial(delta_kernel, heads, head_devs),
        grid_spec=pltpu.PrefetchScalarGridSpec(
            num_scalar_prefetch=1,
            grid=(STEPS,),
            in_specs=[spec, spec, spec, spec, pl.BlockSpec((heads, rows), lambda i, s: (0, i)), spec, whole((1, hd)),
                      whole((heads, hd, hd)), whole((share, tokens)), in_hbm],
            out_specs=[in_hbm, in_hbm, in_hbm],
            scratch_shapes=[pltpu.VMEM((heads, hd, hd), f32), pltpu.VMEM((tokens, width), bf16),
                            pltpu.VMEM((tokens, width), bf16), pltpu.VMEM((tokens, share), f32), pltpu.VMEM((tokens // 2, full), f32),
                            pltpu.VMEM((2, tokens // 2, full), bf16), pltpu.VMEM((width, full), bf16),
                            pltpu.SemaphoreType.DMA, pltpu.SemaphoreType.DMA((3,))],
        ),
        out_shape=[jax.ShapeDtypeStruct((heads, hd, hd), f32), jax.ShapeDtypeStruct((tokens // 2, full), bf16),
                   jax.ShapeDtypeStruct((tokens // 2, full), bf16)],
        compiler_params=pltpu.CompilerParams(vmem_limit_bytes=DELTA_VMEM),
        cost_estimate=cost(2 * tokens * width * full * 3, 8 * MIB),
        name="delta",
    )(scalars, q, k, v, dec, beta, gate, gain, state, resid, w_out)


def pair_kernel(keep, got, own, *sends):
    piece = own.shape[0]
    for i in range(len(sends) + 1):
        r = slice(i * piece, (i + 1) * piece)
        total = keep[r, :].astype(f32) + got[r, :].astype(f32)
        if i == 0:
            own[...] = total
        else:
            sends[i - 1][...] = total.astype(bf16)


def pair_sum(keep, got, chips):
    rows, full = keep.shape
    piece = rows // chips
    return pl.pallas_call(
        pair_kernel,
        in_specs=[pl.BlockSpec(memory_space=pltpu.VMEM)] * 2,
        out_specs=[pl.BlockSpec(memory_space=pltpu.VMEM)] * chips,
        out_shape=[jax.ShapeDtypeStruct((piece, full), f32)]
        + [jax.ShapeDtypeStruct((piece, full), bf16)] * (chips - 1),
        compiler_params=pltpu.CompilerParams(vmem_limit_bytes=10 * MIB),
        cost_estimate=cost(rows * full, rows * full * 8),
        name="pair_sum",
    )(keep, got)


def pace_kernel(place, total, out):
    out[...] = place[...]


def pace(place, total):
    return pl.pallas_call(
        pace_kernel,
        in_specs=[pl.BlockSpec(memory_space=pltpu.VMEM), pl.BlockSpec(memory_space=pl.ANY)],
        out_specs=pl.BlockSpec(memory_space=pltpu.VMEM),
        out_shape=jax.ShapeDtypeStruct(place.shape, place.dtype),
        compiler_params=pltpu.CompilerParams(vmem_limit_bytes=2 * MIB),
        cost_estimate=cost(1.2e10, 0),
        name="pace",
    )(place, total)


def to_chip(x, step, devs):
    return lax.ppermute(x, "head", [(i, (i + 2 * step) % devs) for i in range(devs)])


def to_core(x, devs):
    return lax.ppermute(x, "head", [(i, i ^ 1) for i in range(devs)])


def to_chips(x, devs):
    chips = devs // 2
    got = [to_chip(x, chips - step, devs) for step in range(1, chips)]
    return [x, *got]


def lanes(x, op):
    total = x[:, :128]
    for at in range(128, x.shape[1], 128):
        total = op(total, x[:, at : at + 128])
    return total


def sources(order, me):
    chips = len(order) // 2
    core, chip = lax.rem(me, 2), lax.div(me, 2)
    return [((1 - core) if other else core, lax.rem(chip + step, chips)) for other, step in order]


def validity(source, devs, page, count, cached_len):
    per = page // devs
    lane = lax.broadcasted_iota(jnp.int32, (1, count), 1)
    core, chip = source
    position = lax.div(lane, per) * page + (chip * 2 + core) * per + lax.rem(lane, per)
    return jnp.where(position < cached_len, 0.0, -jnp.inf)


def lay(keys, k_ref):
    at = 0
    for key in keys:
        k_ref[at : at + key.shape[0], :] = key[...]
        at += key.shape[0]


def score(absorbed, widths, biases, k_ref):
    scores, top, at = [], None, 0
    for width, bias in zip(widths, biases):
        s = bias(mm(absorbed, k_ref[at : at + width, :], ((1,), (1,))))
        scores.append(s)
        best = lanes(s, jnp.maximum)
        top = best if top is None else jnp.maximum(top, best)
        at += width
    return scores, top


def attend(scored, state, k_ref, e_ref):
    scores, top = scored
    top = jnp.max(top, axis=1, keepdims=True)
    peak = top if state is None else jnp.maximum(state[0], top)
    total, at = None, 0
    for s in scores:
        e = jnp.exp2(s - peak)
        add = lanes(e, jnp.add)
        total = add if total is None else total + add
        e_ref[:, at : at + s.shape[1]] = e.astype(bf16)
        at += s.shape[1]
    acc = jnp.dot(e_ref[:, :at], k_ref[:at, :], preferred_element_type=f32)
    if state is not None:
        shrink = jnp.exp2(state[0] - peak)
        total = total + state[1] * shrink
        acc = acc + state[2] * shrink
    return peak, total, acc


def front_kernel(heads, order, page, near, sc, *refs):
    n = len(order)
    xs, refs = refs[:n], refs[n:]
    pages, refs = refs[: len(near)], refs[len(near) :]
    w_q, w_dkv, w_uk, gain, latent_gain = refs[:5]
    resid_ref, absorbed_ref, peak_ref, total_ref, acc_ref = refs[5:10]
    x_scr, n_scr, r_scr, l_scr, k_scr, e_scr, q_scr, d_scr, sem = refs[10:]
    fetch = [pltpu.make_async_copy(w_q, q_scr, sem.at[0]), pltpu.make_async_copy(w_dkv, d_scr, sem.at[1])]
    for copy in fetch:
        copy.start()
    rows, full = x_scr.shape
    half, piece = rows // 2, rows // n
    share = resid_ref.shape[0]
    hd = w_uk.shape[1]
    me, cached_len = sc[1], sc[2]
    source = sources(order, me)
    for x, (owner, at) in zip(xs, source):
        x_scr[pl.ds(pl.multiple_of(owner * half + at * piece, piece), piece), :] = x[...]
    for dev in range(n):
        @pl.when(me == dev)
        def _():
            r_scr[...] = x_scr[:, dev * share : (dev + 1) * share]
    eye = lax.broadcasted_iota(jnp.int32, (share, share), 0) == lax.broadcasted_iota(jnp.int32, (share, share), 1)
    resid_ref[...] = mm(eye, r_scr[...], ((1,), (1,))).astype(bf16)
    wide = x_scr[...].astype(f32)
    power = jnp.sum(wide * wide, axis=1, keepdims=True) * (1.0 / full)
    n_scr[...] = (wide * lax.rsqrt(power + EPS) * gain[...]).astype(bf16)
    fetch[0].wait()
    query = jnp.dot(n_scr[...], q_scr[...], preferred_element_type=f32).astype(bf16)
    fetch[1].wait()
    pre = jnp.dot(n_scr[...], d_scr[...], preferred_element_type=f32)
    power = jnp.sum(pre * pre, axis=1, keepdims=True) * (1.0 / pre.shape[1])
    l_scr[...] = (pre * lax.rsqrt(power + EPS) * latent_gain[...]).astype(bf16)
    count = pages[0].shape[0]
    valid = [validity(source[i], n, page, count, cached_len) for i in near]
    biases = [lambda s, v=v: s + v for v in valid]
    causal = lax.broadcasted_iota(jnp.int32, (rows, rows), 1) <= lax.broadcasted_iota(jnp.int32, (rows, rows), 0)
    biases.append(lambda s: jnp.where(causal, s, -jnp.inf))
    scale = math.log2(math.e) / math.sqrt(hd)
    keys = [*pages, l_scr]
    lay(keys, k_scr)
    widths = [key.shape[0] for key in keys]

    def scores_of(h):
        rs = slice(h * rows, (h + 1) * rows)
        absorbed = jnp.dot(query[:, h * hd : (h + 1) * hd], w_uk[h], preferred_element_type=f32) * scale
        absorbed_ref[rs, :] = absorbed.astype(bf16)
        return score(absorbed_ref[rs, :], widths, biases, k_scr)

    scored = scores_of(0)
    for h in range(heads):
        rs = slice(h * rows, (h + 1) * rows)
        later = scores_of(h + 1) if h + 1 < heads else None
        peak, total, acc = attend(scored, None, k_scr, e_scr.at[h % 2])
        scored = later
        peak_ref[rs, :] = jnp.broadcast_to(peak, total.shape)
        total_ref[rs, :] = total
        acc_ref[rs, :] = acc.astype(bf16)


def front(order, near, page, scalars, xs, pages, w_q, w_dkv, w_uk, gain, latent_gain):
    heads, hd, lat = w_uk.shape
    rows, full = xs[0].shape[0] * len(xs), xs[0].shape[1]
    share = full // len(xs)
    args = [*xs, *pages, w_q, w_dkv, w_uk, gain, latent_gain]
    keys = pages[0].shape[0] * len(near) + rows
    in_vmem = pl.BlockSpec(memory_space=pltpu.VMEM)
    return pl.pallas_call(
        functools.partial(front_kernel, heads, order, page, near),
        grid_spec=pltpu.PrefetchScalarGridSpec(
            num_scalar_prefetch=1,
            grid=(1,),
            in_specs=[in_vmem] * (len(args) - 5) + [pl.BlockSpec(memory_space=pl.ANY)] * 2 + [in_vmem] * 3,
            out_specs=[whole((share, rows))] + [in_vmem] * 4,
            scratch_shapes=[pltpu.VMEM((rows, full), bf16), pltpu.VMEM((rows, full), bf16),
                            pltpu.VMEM((rows, share), bf16), pltpu.VMEM((rows, lat), bf16),
                            pltpu.VMEM((keys, lat), bf16), pltpu.VMEM((2, rows, keys), bf16),
                            pltpu.VMEM((full, heads * hd), bf16), pltpu.VMEM((full, lat), bf16),
                            pltpu.SemaphoreType.DMA((2,))],
        ),
        out_shape=[jax.ShapeDtypeStruct((share, rows), bf16), jax.ShapeDtypeStruct((heads * rows, lat), bf16),
                   jax.ShapeDtypeStruct((heads * rows, 128), f32), jax.ShapeDtypeStruct((heads * rows, 128), f32),
                   jax.ShapeDtypeStruct((heads * rows, lat), bf16)],
        compiler_params=pltpu.CompilerParams(vmem_limit_bytes=FRONT_VMEM),
        cost_estimate=cost(2 * rows * (full * 2 * lat + heads * lat * (hd + 2 * keys)), 12 * MIB),
        name="front",
    )(scalars, *args)


def back_kernel(heads, order, page, far, sc, *refs):
    absorbed_ref, peak_ref, total_ref, acc_ref, refs = *refs[:4], refs[4:]
    pages, refs = refs[: len(far)], refs[len(far) :]
    w_uv, out_ref, k_scr, e_scr = refs
    rows = out_ref.shape[0]
    hd = w_uv.shape[2]
    new_len, me, cached_len = sc[0], sc[1], sc[2]
    source = sources(order, me)
    count = pages[0].shape[0]
    valid = [validity(source[i], len(order), page, count, cached_len) for i in far]
    biases = [lambda s, v=v: s + v for v in valid]
    live = lax.broadcasted_iota(jnp.int32, (rows, hd), 0) < new_len
    lay(pages, k_scr)
    widths = [count] * len(pages)
    scored = score(absorbed_ref[:rows, :], widths, biases, k_scr)
    for h in range(heads):
        rs = slice(h * rows, (h + 1) * rows)
        later = score(absorbed_ref[(h + 1) * rows : (h + 2) * rows, :], widths, biases, k_scr) if h + 1 < heads else None
        state = peak_ref[rs, 0:1], total_ref[rs, :], acc_ref[rs, :].astype(f32)
        _, total, acc = attend(scored, state, k_scr, e_scr.at[h % 2])
        scored = later
        attended = (acc / jnp.sum(total, axis=1, keepdims=True)).astype(bf16)
        value = jnp.dot(attended, w_uv[h], preferred_element_type=f32)
        out_ref[:, h * hd : (h + 1) * hd] = jnp.where(live, value, 0.0).astype(bf16)


def back(order, far, page, scalars, state, pages, w_uv):
    heads, lat, hd = w_uv.shape
    rows = state[0].shape[0] // heads
    args = [*state, *pages, w_uv]
    keys = pages[0].shape[0] * len(far)
    return pl.pallas_call(
        functools.partial(back_kernel, heads, order, page, far),
        grid_spec=pltpu.PrefetchScalarGridSpec(
            num_scalar_prefetch=1,
            grid=(1,),
            in_specs=[pl.BlockSpec(memory_space=pltpu.VMEM)] * len(args),
            out_specs=whole((rows, heads * hd)),
            scratch_shapes=[pltpu.VMEM((keys, lat), bf16), pltpu.VMEM((2, rows, keys), bf16)],
        ),
        out_shape=jax.ShapeDtypeStruct((rows, heads * hd), bf16),
        compiler_params=pltpu.CompilerParams(vmem_limit_bytes=LATENT_VMEM),
        cost_estimate=cost(2 * rows * heads * lat * (hd + 2 * keys), 12 * MIB),
        name="back",
    )(scalars, *args)


def listed_rows(page_owner, page_slot, pool, me, devs):
    here = lax.axis_index("batch")
    owners = lax.axis_size("batch")
    page_count = page_owner.shape[1]
    most = max(2, 2 * page_count // owners)
    per = pool.shape[1] // devs
    before = jnp.arange(page_count, dtype=jnp.int32)
    earlier = before[None, :] < before[:, None]
    hits = page_owner == here
    ranks = jnp.sum((hits[:, None, :] & earlier[None]).astype(jnp.int32), axis=2)
    chosen = hits[:, None, :] & (ranks[:, None, :] == jnp.arange(most, dtype=jnp.int32)[None, :, None])
    wanted = jnp.sum(jnp.where(chosen, page_slot[:, None, :], 0), axis=2)
    rows = lax.dynamic_slice_in_dim(pool, me * per, per, 1)
    outgoing = jnp.take(rows, wanted, axis=0, mode="clip")
    mine = lax.dynamic_index_in_dim(page_owner, here, 0, keepdims=False)
    rank = jnp.sum(((mine[:, None] == mine[None, :]) & earlier).astype(jnp.int32), axis=1)
    return outgoing, mine * most + rank


def pick_kernel(place, flat, out, sem):
    copies = [pltpu.make_async_copy(flat.at[place[i]], out.at[i], sem.at[i]) for i in range(out.shape[0])]
    for copy in copies:
        copy.start()
    for copy in copies:
        copy.wait()


def pick(place, flat):
    return pl.pallas_call(
        pick_kernel,
        grid_spec=pltpu.PrefetchScalarGridSpec(
            num_scalar_prefetch=1,
            grid=(1,),
            in_specs=[pl.BlockSpec(memory_space=pl.ANY)],
            out_specs=pl.BlockSpec(memory_space=pltpu.VMEM),
            scratch_shapes=[pltpu.SemaphoreType.DMA(place.shape)],
        ),
        out_shape=jax.ShapeDtypeStruct(place.shape + flat.shape[1:], flat.dtype),
        compiler_params=pltpu.CompilerParams(vmem_limit_bytes=2 * MIB),
        cost_estimate=cost(0, place.shape[0] * flat[0].size * 4),
        name="pick",
    )(place, flat)


def on_device(
    resid_in, kda_q, kda_k, kda_v, log_decay, beta, out_gate, kda_gain, kda_state, w_out_kda, mla_gain,
    w_q, w_uk, w_dkv, latent_gain, latent_pool, page_owner, page_slot, cached_len, new_len, w_uv,
):
    devs = lax.axis_size("head")
    chips = devs // 2
    me = lax.axis_index("head")
    scalars = jnp.stack([new_len[0], me.astype(jnp.int32), cached_len[0]])
    page = latent_pool.shape[1]

    state, keep, other = delta(
        devs, scalars, kda_q, kda_k, kda_v, log_decay, beta.T, out_gate, kda_gain.reshape(1, -1),
        kda_state[0], resid_in.T, w_out_kda
    )
    got = to_core(other, devs)
    outgoing, place = listed_rows(page_owner, page_slot, latent_pool, me, devs)
    own, *sends = pair_sum(keep, got, chips)
    sends, outgoing = lax.optimization_barrier((sends, outgoing))
    got = [to_chip(send, step + 1, devs) for step, send in enumerate(sends)]
    arrived = lax.all_to_all(outgoing, "batch", split_axis=0, concat_axis=0, tiled=True)
    flat = arrived.reshape((-1,) + arrived.shape[2:])

    total = own
    for part in got:
        total = total + part.astype(f32)
    total = total.astype(bf16)
    x_here = to_chips(total, devs)
    place = pace(place, total)
    my_rows = pick(place, flat).reshape(-1, latent_pool.shape[2])
    pages_here = to_chips(my_rows, devs)
    near_page = to_core(my_rows, devs)
    x_here[1:], near_page = lax.optimization_barrier((x_here[1:], near_page))
    xs = x_here + [to_core(x, devs) for x in x_here]
    order = [(0, step) for step in range(chips)] + [(1, step) for step in range(chips)]
    near, far = [0, chips], [i for i in range(devs) if i % chips]
    resid_mid, *held = front(
        order, near, page, scalars, xs, [my_rows, near_page], w_q, w_dkv, w_uk, mla_gain.reshape(1, -1),
        latent_gain.reshape(1, -1)
    )
    others, resid_mid = lax.optimization_barrier((pages_here[1:], resid_mid))
    mla_out = back(order, far, page, scalars, held, others + [to_core(p, devs) for p in others], w_uv)
    return (resid_mid.T, state[None], mla_out)


def solution(mesh):
    in_specs = (
        P("batch", "head"),
        P("batch", "head"),
        P("batch", "head"),
        P("batch", "head"),
        P("batch", "head"),
        P("batch", "head"),
        P("batch", "head"),
        P(),
        P("batch", "head", None, None),
        P("head", None),
        P(),
        P(None, "head"),
        P("head", None, None),
        P(),
        P(),
        P("batch", None, None),
        P(),
        P(),
        P("batch"),
        P("batch"),
        P("head", None, None),
    )
    out_specs = (P("batch", "head"), P("batch", "head", None, None), P("batch", "head"))
    return jax.shard_map(
        on_device, mesh=mesh, in_specs=in_specs, out_specs=out_specs, check_vma=False
    )
```

```python
import functools
import math

import jax
import jax.numpy as jnp
from jax import lax
from jax.experimental import pallas as pl
from jax.experimental.pallas import tpu as pltpu
from jax.sharding import PartitionSpec as P

f32, bf16 = jnp.float32, jnp.bfloat16
EPS = 1e-6
CHUNK = 64
TILE = 128
STEPS = 2
MIB = 2**20
DELTA_VMEM = 56 * MIB
FRONT_VMEM = 43 * MIB
LATENT_VMEM = 20 * MIB


def mm(a, b, dims=((1,), (0,))):
    return lax.dot_general(
        a.astype(bf16), b.astype(bf16), (dims, ((), ())), preferred_element_type=f32
    )


def cost(flops, nbytes):
    return pl.CostEstimate(flops=int(flops), bytes_accessed=int(nbytes), transcendentals=0)


def whole(shape):
    return pl.BlockSpec(shape, lambda *_: (0,) * len(shape))


def delta_tokens(heads, first_row, new_len, q_ref, k_ref, v_ref, d_ref, b_ref, g_ref, gain, s_ref, store):
    rows = q_ref.shape[0]
    hd = s_ref.shape[-1]
    ri = lax.broadcasted_iota(jnp.int32, (TILE, TILE), 0)
    ci = lax.broadcasted_iota(jnp.int32, (TILE, TILE), 1)
    same = (ri // CHUNK) == (ci // CHUNK)
    lower = same & (ri >= ci)
    strict = same & (ri > ci)
    eye = (ri == ci).astype(f32)
    tri = lower.astype(bf16)
    levels = []
    b = 2
    while b <= CHUNK:
        half = b // 2
        levels.append(((ri // b) == (ci // b)) & ((ri // half) % 2 == 1) & ((ci // half) % 2 == 0))
        b *= 2
    tiles = rows // TILE
    work = [(t, h) for t in range(tiles) for h in range(heads)]
    row_id = lax.broadcasted_iota(jnp.int32, (TILE, hd), 0)
    lives = [(row_id + (first_row + t * TILE)) < new_len for t in range(tiles)]
    st = {}
    for t, h in work:
        rs = slice(t * TILE, (t + 1) * TILE)
        cs = slice(h * hd, (h + 1) * hd)
        live = lives[t]
        q = q_ref[rs, cs].astype(f32)
        k = k_ref[rs, cs].astype(f32)
        v = v_ref[rs, cs].astype(f32)
        dec = jnp.where(live, d_ref[rs, cs], 0.0)
        hi = dec.astype(bf16)
        lo = (dec - hi.astype(f32)).astype(bf16)
        cum = mm(tri, hi) + mm(tri, lo)
        beta = jnp.where(live, jnp.broadcast_to(b_ref[h : h + 1, rs], (hd, TILE)).T, 0.0)
        q = q * (lax.rsqrt(jnp.sum(q * q, axis=1, keepdims=True) + EPS) * (1.0 / math.sqrt(hd)))
        k = k * lax.rsqrt(jnp.sum(k * k, axis=1, keepdims=True) + EPS)
        grown = jnp.exp(cum)
        ke = k * grown
        qe = (q * grown).astype(bf16)
        kit = (k * jnp.exp(-cum)).T.astype(bf16)
        pair = mm(jnp.concatenate([ke.astype(bf16), qe], 0), kit)
        kk = jnp.where(strict, pair[:TILE], 0.0) * beta
        qk = jnp.where(lower, pair[TILE:], 0.0).astype(bf16)
        rhs = jnp.concatenate([(ke * beta).astype(bf16), (v * beta).astype(bf16)], 1)
        lasts = [
            jnp.broadcast_to(grown[(j + 1) * CHUNK - 1 : (j + 1) * CHUNK, :], (hd, hd)).T
            for j in range(TILE // CHUNK)
        ]
        st[t, h] = (kk, rhs, kit, qe, qk, lasts)
    invs = {w: eye - jnp.where(levels[0], st[w][0], 0.0) for w in work}
    for level in levels[1:]:
        left = {w: mm(invs[w], jnp.where(level, st[w][0], 0.0)) for w in work}
        invs = {w: invs[w] - mm(left[w], invs[w]) for w in work}
    solved = {w: mm(invs[w], st[w][1]) for w in work}
    state = [s_ref[h] for h in range(heads)]
    outs = {}
    for t in range(tiles):
        for j in range(TILE // CHUNK):
            r = slice(j * CHUNK, (j + 1) * CHUNK)
            seen = [
                mm(jnp.concatenate([solved[t, h][r, :hd].astype(bf16), st[t, h][3][r]], 0), state[h])
                for h in range(heads)
            ]
            for h in range(heads):
                _, _, kit, _, qk, lasts = st[t, h]
                fresh = solved[t, h][r, hd:] - seen[h][:CHUNK]
                outs[t, h, j] = seen[h][CHUNK:] + mm(qk[r, r], fresh)
                state[h] = lasts[j] * (state[h] + mm(kit[:, r], fresh))
    for h in range(heads):
        s_ref[h] = state[h]
    for t, h in work:
        rs = slice(t * TILE, (t + 1) * TILE)
        cs = slice(h * hd, (h + 1) * hd)
        o = jnp.concatenate([outs[t, h, j] for j in range(TILE // CHUNK)], 0)
        scale = lax.rsqrt(jnp.sum(o * o, axis=1, keepdims=True) * (1.0 / hd) + EPS)
        gate = 1.0 / (1.0 + jnp.exp(-g_ref[rs, cs].astype(f32)))
        store(rs, cs, jnp.where(lives[t], o * scale * gain * gate, 0.0).astype(bf16))


def delta_kernel(heads, head_devs, sc, q, k, v, d, b, g, gain, s0, resid, w_hbm,
                 s_out, keep_ref, other_ref, s_ref, mix_scr, ord_scr, res_scr, sum_scr, out_scr, w_scr, sem, out_sem):
    step = pl.program_id(0)
    rows = q.shape[0]
    tokens = mix_scr.shape[0]
    half, piece = tokens // 2, tokens // head_devs
    share = resid.shape[0]
    me = sc[1]
    chips = head_devs // 2
    core, chip = lax.rem(me, 2), lax.div(me, 2)

    @pl.when(step == 0)
    def _():
        pltpu.make_async_copy(w_hbm, w_scr, sem).start()
        s_ref[...] = s0[...]

    def store(rs, cs, value):
        mix_scr[pl.ds(pl.multiple_of(step * rows + rs.start, TILE), TILE), cs] = value

    delta_tokens(heads, step * rows, sc[0], q, k, v, d, b, g, gain[...], s_ref, store)

    @pl.when(step == pl.num_programs(0) - 1)
    def _():
        for part in range(2):
            owner = (1 - core) if part == 0 else core
            for i in range(chips):
                at = pl.multiple_of(owner * half + lax.rem(chip + i, chips) * piece, piece)
                to = slice(part * half + i * piece, part * half + (i + 1) * piece)
                ord_scr[to, :] = mix_scr[pl.ds(at, piece), :]
        to = lax.broadcasted_iota(jnp.int32, (tokens, 1), 0)
        at = lax.broadcasted_iota(jnp.int32, (tokens, tokens), 1)
        owner = jnp.where(to < half, 1 - core, core)
        turn = lax.rem(chip + lax.div(lax.rem(to, half), piece), chips)
        order = (at == owner * half + turn * piece + lax.rem(to, piece)).astype(bf16)
        res_scr[...] = mm(order, resid[...], ((1,), (1,)))
        pltpu.make_async_copy(w_hbm, w_scr, sem).wait()
        copies = [pltpu.make_async_copy(s_ref, s_out, out_sem.at[2])]
        copies[0].start()
        for part, ref in enumerate((other_ref, keep_ref)):
            rs = slice(part * half, (part + 1) * half)
            sum_scr[...] = jnp.dot(ord_scr[rs], w_scr[...], preferred_element_type=f32)
            for dev in range(head_devs):
                @pl.when(me == dev)
                def _():
                    @pl.loop(0, chips)
                    def _(i):
                        at = pl.multiple_of(i * piece, piece)
                        sum_scr[pl.ds(at, piece), dev * share : (dev + 1) * share] += res_scr[
                            pl.ds(pl.multiple_of(part * half + at, piece), piece), :
                        ]
            out_scr[part] = sum_scr[...].astype(bf16)
            copies.append(pltpu.make_async_copy(out_scr.at[part], ref, out_sem.at[part]))
            copies[-1].start()
        for copy in copies:
            copy.wait()


def delta(head_devs, scalars, q, k, v, dec, beta, gate, gain, state, resid, w_out):
    tokens, width = q.shape
    heads = beta.shape[0]
    hd = width // heads
    rows = tokens // STEPS
    share = resid.shape[0]
    full = w_out.shape[1]
    spec = pl.BlockSpec((rows, width), lambda i, s: (i, 0))
    in_hbm = pl.BlockSpec(memory_space=pl.ANY)
    return pl.pallas_call(
        functools.partial(delta_kernel, heads, head_devs),
        grid_spec=pltpu.PrefetchScalarGridSpec(
            num_scalar_prefetch=1,
            grid=(STEPS,),
            in_specs=[spec, spec, spec, spec, pl.BlockSpec((heads, rows), lambda i, s: (0, i)), spec, whole((1, hd)),
                      whole((heads, hd, hd)), whole((share, tokens)), in_hbm],
            out_specs=[in_hbm, in_hbm, in_hbm],
            scratch_shapes=[pltpu.VMEM((heads, hd, hd), f32), pltpu.VMEM((tokens, width), bf16),
                            pltpu.VMEM((tokens, width), bf16), pltpu.VMEM((tokens, share), f32), pltpu.VMEM((tokens // 2, full), f32),
                            pltpu.VMEM((2, tokens // 2, full), bf16), pltpu.VMEM((width, full), bf16),
                            pltpu.SemaphoreType.DMA, pltpu.SemaphoreType.DMA((3,))],
        ),
        out_shape=[jax.ShapeDtypeStruct((heads, hd, hd), f32), jax.ShapeDtypeStruct((tokens // 2, full), bf16),
                   jax.ShapeDtypeStruct((tokens // 2, full), bf16)],
        compiler_params=pltpu.CompilerParams(vmem_limit_bytes=DELTA_VMEM),
        cost_estimate=cost(2 * tokens * width * full * 3, 8 * MIB),
        name="delta",
    )(scalars, q, k, v, dec, beta, gate, gain, state, resid, w_out)


def pair_kernel(keep, got, own, *sends):
    piece = own.shape[0]
    for i in range(len(sends) + 1):
        r = slice(i * piece, (i + 1) * piece)
        total = keep[r, :].astype(f32) + got[r, :].astype(f32)
        if i == 0:
            own[...] = total
        else:
            sends[i - 1][...] = total.astype(bf16)


def pair_sum(keep, got, chips):
    rows, full = keep.shape
    piece = rows // chips
    return pl.pallas_call(
        pair_kernel,
        in_specs=[pl.BlockSpec(memory_space=pltpu.VMEM)] * 2,
        out_specs=[pl.BlockSpec(memory_space=pltpu.VMEM)] * chips,
        out_shape=[jax.ShapeDtypeStruct((piece, full), f32)]
        + [jax.ShapeDtypeStruct((piece, full), bf16)] * (chips - 1),
        compiler_params=pltpu.CompilerParams(vmem_limit_bytes=10 * MIB),
        cost_estimate=cost(rows * full, rows * full * 8),
        name="pair_sum",
    )(keep, got)


def pace_kernel(place, total, out):
    out[...] = place[...]


def pace(place, total):
    return pl.pallas_call(
        pace_kernel,
        in_specs=[pl.BlockSpec(memory_space=pltpu.VMEM), pl.BlockSpec(memory_space=pl.ANY)],
        out_specs=pl.BlockSpec(memory_space=pltpu.VMEM),
        out_shape=jax.ShapeDtypeStruct(place.shape, place.dtype),
        compiler_params=pltpu.CompilerParams(vmem_limit_bytes=2 * MIB),
        cost_estimate=cost(1.2e10, 0),
        name="pace",
    )(place, total)


def to_chip(x, step, devs):
    return lax.ppermute(x, "head", [(i, (i + 2 * step) % devs) for i in range(devs)])


def to_core(x, devs):
    return lax.ppermute(x, "head", [(i, i ^ 1) for i in range(devs)])


def to_chips(x, devs):
    chips = devs // 2
    got = [to_chip(x, chips - step, devs) for step in range(1, chips)]
    return [x, *got]


def lanes(x, op):
    total = x[:, :128]
    for at in range(128, x.shape[1], 128):
        total = op(total, x[:, at : at + 128])
    return total


def sources(order, me):
    chips = len(order) // 2
    core, chip = lax.rem(me, 2), lax.div(me, 2)
    return [((1 - core) if other else core, lax.rem(chip + step, chips)) for other, step in order]


def validity(source, devs, page, count, cached_len):
    per = page // devs
    lane = lax.broadcasted_iota(jnp.int32, (1, count), 1)
    core, chip = source
    position = lax.div(lane, per) * page + (chip * 2 + core) * per + lax.rem(lane, per)
    return jnp.where(position < cached_len, 0.0, -jnp.inf)


def lay(keys, k_ref):
    at = 0
    for key in keys:
        k_ref[at : at + key.shape[0], :] = key[...]
        at += key.shape[0]


def score(absorbed, widths, biases, k_ref):
    scores, top, at = [], None, 0
    for width, bias in zip(widths, biases):
        s = bias(mm(absorbed, k_ref[at : at + width, :], ((1,), (1,))))
        scores.append(s)
        best = lanes(s, jnp.maximum)
        top = best if top is None else jnp.maximum(top, best)
        at += width
    return scores, top


def attend(scored, state, k_ref, e_ref):
    scores, top = scored
    top = jnp.max(top, axis=1, keepdims=True)
    peak = top if state is None else jnp.maximum(state[0], top)
    total, at = None, 0
    for s in scores:
        e = jnp.exp2(s - peak)
        add = lanes(e, jnp.add)
        total = add if total is None else total + add
        e_ref[:, at : at + s.shape[1]] = e.astype(bf16)
        at += s.shape[1]
    acc = jnp.dot(e_ref[:, :at], k_ref[:at, :], preferred_element_type=f32)
    if state is not None:
        shrink = jnp.exp2(state[0] - peak)
        total = total + state[1] * shrink
        acc = acc + state[2] * shrink
    return peak, total, acc


def front_kernel(heads, order, page, near, sc, *refs):
    n = len(order)
    xs, refs = refs[:n], refs[n:]
    pages, refs = refs[: len(near)], refs[len(near) :]
    w_q, w_dkv, w_uk, gain, latent_gain = refs[:5]
    resid_ref, absorbed_ref, peak_ref, total_ref, acc_ref = refs[5:10]
    x_scr, n_scr, r_scr, l_scr, k_scr, e_scr, q_scr, d_scr, sem = refs[10:]
    fetch = [pltpu.make_async_copy(w_q, q_scr, sem.at[0]), pltpu.make_async_copy(w_dkv, d_scr, sem.at[1])]
    for copy in fetch:
        copy.start()
    rows, full = x_scr.shape
    half, piece = rows // 2, rows // n
    share = resid_ref.shape[0]
    hd = w_uk.shape[1]
    me, cached_len = sc[1], sc[2]
    source = sources(order, me)
    for x, (owner, at) in zip(xs, source):
        x_scr[pl.ds(pl.multiple_of(owner * half + at * piece, piece), piece), :] = x[...]
    for dev in range(n):
        @pl.when(me == dev)
        def _():
            @pl.loop(0, n)
            def _(i):
                at = pl.ds(pl.multiple_of(i * piece, piece), piece)
                r_scr[at, :] = x_scr[at, dev * share : (dev + 1) * share]
    eye = lax.broadcasted_iota(jnp.int32, (share, share), 0) == lax.broadcasted_iota(jnp.int32, (share, share), 1)
    resid_ref[...] = mm(eye, r_scr[...], ((1,), (1,))).astype(bf16)
    wide = x_scr[...].astype(f32)
    power = jnp.sum(wide * wide, axis=1, keepdims=True) * (1.0 / full)
    n_scr[...] = (wide * lax.rsqrt(power + EPS) * gain[...]).astype(bf16)
    fetch[0].wait()
    query = jnp.dot(n_scr[...], q_scr[...], preferred_element_type=f32).astype(bf16)
    fetch[1].wait()
    pre = jnp.dot(n_scr[...], d_scr[...], preferred_element_type=f32)
    power = jnp.sum(pre * pre, axis=1, keepdims=True) * (1.0 / pre.shape[1])
    l_scr[...] = (pre * lax.rsqrt(power + EPS) * latent_gain[...]).astype(bf16)
    count = pages[0].shape[0]
    valid = [validity(source[i], n, page, count, cached_len) for i in near]
    biases = [lambda s, v=v: s + v for v in valid]
    causal = lax.broadcasted_iota(jnp.int32, (rows, rows), 1) <= lax.broadcasted_iota(jnp.int32, (rows, rows), 0)
    biases.append(lambda s: jnp.where(causal, s, -jnp.inf))
    scale = math.log2(math.e) / math.sqrt(hd)
    keys = [*pages, l_scr]
    lay(keys, k_scr)
    widths = [key.shape[0] for key in keys]

    def scores_of(h):
        rs = slice(h * rows, (h + 1) * rows)
        absorbed = jnp.dot(query[:, h * hd : (h + 1) * hd], w_uk[h], preferred_element_type=f32) * scale
        absorbed_ref[rs, :] = absorbed.astype(bf16)
        return score(absorbed_ref[rs, :], widths, biases, k_scr)

    scored = scores_of(0)
    for h in range(heads):
        rs = slice(h * rows, (h + 1) * rows)
        later = scores_of(h + 1) if h + 1 < heads else None
        peak, total, acc = attend(scored, None, k_scr, e_scr.at[h % 2])
        scored = later
        peak_ref[rs, :] = jnp.broadcast_to(peak, total.shape)
        total_ref[rs, :] = total
        acc_ref[rs, :] = acc.astype(bf16)


def front(order, near, page, scalars, xs, pages, w_q, w_dkv, w_uk, gain, latent_gain):
    heads, hd, lat = w_uk.shape
    rows, full = xs[0].shape[0] * len(xs), xs[0].shape[1]
    share = full // len(xs)
    args = [*xs, *pages, w_q, w_dkv, w_uk, gain, latent_gain]
    keys = pages[0].shape[0] * len(near) + rows
    in_vmem = pl.BlockSpec(memory_space=pltpu.VMEM)
    return pl.pallas_call(
        functools.partial(front_kernel, heads, order, page, near),
        grid_spec=pltpu.PrefetchScalarGridSpec(
            num_scalar_prefetch=1,
            grid=(1,),
            in_specs=[in_vmem] * (len(args) - 5) + [pl.BlockSpec(memory_space=pl.ANY)] * 2 + [in_vmem] * 3,
            out_specs=[whole((share, rows))] + [in_vmem] * 4,
            scratch_shapes=[pltpu.VMEM((rows, full), bf16), pltpu.VMEM((rows, full), bf16),
                            pltpu.VMEM((rows, share), bf16), pltpu.VMEM((rows, lat), bf16),
                            pltpu.VMEM((keys, lat), bf16), pltpu.VMEM((2, rows, keys), bf16),
                            pltpu.VMEM((full, heads * hd), bf16), pltpu.VMEM((full, lat), bf16),
                            pltpu.SemaphoreType.DMA((2,))],
        ),
        out_shape=[jax.ShapeDtypeStruct((share, rows), bf16), jax.ShapeDtypeStruct((heads * rows, lat), bf16),
                   jax.ShapeDtypeStruct((heads * rows, 128), f32), jax.ShapeDtypeStruct((heads * rows, 128), f32),
                   jax.ShapeDtypeStruct((heads * rows, lat), bf16)],
        compiler_params=pltpu.CompilerParams(vmem_limit_bytes=FRONT_VMEM),
        cost_estimate=cost(2 * rows * (full * 2 * lat + heads * lat * (hd + 2 * keys)), 12 * MIB),
        name="front",
    )(scalars, *args)


def back_kernel(heads, order, page, far, sc, *refs):
    absorbed_ref, peak_ref, total_ref, acc_ref, refs = *refs[:4], refs[4:]
    pages, refs = refs[: len(far)], refs[len(far) :]
    w_uv, out_ref, k_scr, e_scr = refs
    rows = out_ref.shape[0]
    hd = w_uv.shape[2]
    new_len, me, cached_len = sc[0], sc[1], sc[2]
    source = sources(order, me)
    count = pages[0].shape[0]
    valid = [validity(source[i], len(order), page, count, cached_len) for i in far]
    biases = [lambda s, v=v: s + v for v in valid]
    live = lax.broadcasted_iota(jnp.int32, (rows, hd), 0) < new_len
    lay(pages, k_scr)
    widths = [count] * len(pages)
    scored = score(absorbed_ref[:rows, :], widths, biases, k_scr)
    for h in range(heads):
        rs = slice(h * rows, (h + 1) * rows)
        later = score(absorbed_ref[(h + 1) * rows : (h + 2) * rows, :], widths, biases, k_scr) if h + 1 < heads else None
        state = peak_ref[rs, 0:1], total_ref[rs, :], acc_ref[rs, :].astype(f32)
        _, total, acc = attend(scored, state, k_scr, e_scr.at[h % 2])
        scored = later
        attended = (acc / jnp.sum(total, axis=1, keepdims=True)).astype(bf16)
        value = jnp.dot(attended, w_uv[h], preferred_element_type=f32)
        out_ref[:, h * hd : (h + 1) * hd] = jnp.where(live, value, 0.0).astype(bf16)


def back(order, far, page, scalars, state, pages, w_uv):
    heads, lat, hd = w_uv.shape
    rows = state[0].shape[0] // heads
    args = [*state, *pages, w_uv]
    keys = pages[0].shape[0] * len(far)
    return pl.pallas_call(
        functools.partial(back_kernel, heads, order, page, far),
        grid_spec=pltpu.PrefetchScalarGridSpec(
            num_scalar_prefetch=1,
            grid=(1,),
            in_specs=[pl.BlockSpec(memory_space=pltpu.VMEM)] * len(args),
            out_specs=whole((rows, heads * hd)),
            scratch_shapes=[pltpu.VMEM((keys, lat), bf16), pltpu.VMEM((2, rows, keys), bf16)],
        ),
        out_shape=jax.ShapeDtypeStruct((rows, heads * hd), bf16),
        compiler_params=pltpu.CompilerParams(vmem_limit_bytes=LATENT_VMEM),
        cost_estimate=cost(2 * rows * heads * lat * (hd + 2 * keys), 12 * MIB),
        name="back",
    )(scalars, *args)


def listed_rows(page_owner, page_slot, pool, me, devs):
    here = lax.axis_index("batch")
    owners = lax.axis_size("batch")
    page_count = page_owner.shape[1]
    most = max(2, 2 * page_count // owners)
    per = pool.shape[1] // devs
    before = jnp.arange(page_count, dtype=jnp.int32)
    earlier = before[None, :] < before[:, None]
    hits = page_owner == here
    ranks = jnp.sum((hits[:, None, :] & earlier[None]).astype(jnp.int32), axis=2)
    chosen = hits[:, None, :] & (ranks[:, None, :] == jnp.arange(most, dtype=jnp.int32)[None, :, None])
    wanted = jnp.sum(jnp.where(chosen, page_slot[:, None, :], 0), axis=2)
    rows = lax.dynamic_slice_in_dim(pool, me * per, per, 1)
    outgoing = jnp.take(rows, wanted, axis=0, mode="clip")
    mine = lax.dynamic_index_in_dim(page_owner, here, 0, keepdims=False)
    rank = jnp.sum(((mine[:, None] == mine[None, :]) & earlier).astype(jnp.int32), axis=1)
    return outgoing, mine * most + rank


def pick_kernel(place, flat, out, sem):
    copies = [pltpu.make_async_copy(flat.at[place[i]], out.at[i], sem.at[i]) for i in range(out.shape[0])]
    for copy in copies:
        copy.start()
    for copy in copies:
        copy.wait()


def pick(place, flat):
    return pl.pallas_call(
        pick_kernel,
        grid_spec=pltpu.PrefetchScalarGridSpec(
            num_scalar_prefetch=1,
            grid=(1,),
            in_specs=[pl.BlockSpec(memory_space=pl.ANY)],
            out_specs=pl.BlockSpec(memory_space=pltpu.VMEM),
            scratch_shapes=[pltpu.SemaphoreType.DMA(place.shape)],
        ),
        out_shape=jax.ShapeDtypeStruct(place.shape + flat.shape[1:], flat.dtype),
        compiler_params=pltpu.CompilerParams(vmem_limit_bytes=2 * MIB),
        cost_estimate=cost(0, place.shape[0] * flat[0].size * 4),
        name="pick",
    )(place, flat)


def on_device(
    resid_in, kda_q, kda_k, kda_v, log_decay, beta, out_gate, kda_gain, kda_state, w_out_kda, mla_gain,
    w_q, w_uk, w_dkv, latent_gain, latent_pool, page_owner, page_slot, cached_len, new_len, w_uv,
):
    devs = lax.axis_size("head")
    chips = devs // 2
    me = lax.axis_index("head")
    scalars = jnp.stack([new_len[0], me.astype(jnp.int32), cached_len[0]])
    page = latent_pool.shape[1]

    state, keep, other = delta(
        devs, scalars, kda_q, kda_k, kda_v, log_decay, beta.T, out_gate, kda_gain.reshape(1, -1),
        kda_state[0], resid_in.T, w_out_kda
    )
    got = to_core(other, devs)
    outgoing, place = listed_rows(page_owner, page_slot, latent_pool, me, devs)
    own, *sends = pair_sum(keep, got, chips)
    sends, outgoing = lax.optimization_barrier((sends, outgoing))
    got = [to_chip(send, step + 1, devs) for step, send in enumerate(sends)]
    arrived = lax.all_to_all(outgoing, "batch", split_axis=0, concat_axis=0, tiled=True)
    flat = arrived.reshape((-1,) + arrived.shape[2:])

    total = own
    for part in got:
        total = total + part.astype(f32)
    total = total.astype(bf16)
    x_here = to_chips(total, devs)
    place = pace(place, total)
    my_rows = pick(place, flat).reshape(-1, latent_pool.shape[2])
    pages_here = to_chips(my_rows, devs)
    near_page = to_core(my_rows, devs)
    x_here[1:], near_page = lax.optimization_barrier((x_here[1:], near_page))
    xs = x_here + [to_core(x, devs) for x in x_here]
    order = [(0, step) for step in range(chips)] + [(1, step) for step in range(chips)]
    near, far = [0, chips], [i for i in range(devs) if i % chips]
    resid_mid, *held = front(
        order, near, page, scalars, xs, [my_rows, near_page], w_q, w_dkv, w_uk, mla_gain.reshape(1, -1),
        latent_gain.reshape(1, -1)
    )
    others, resid_mid = lax.optimization_barrier((pages_here[1:], resid_mid))
    mla_out = back(order, far, page, scalars, held, others + [to_core(p, devs) for p in others], w_uv)
    return (resid_mid.T, state[None], mla_out)


def solution(mesh):
    in_specs = (
        P("batch", "head"),
        P("batch", "head"),
        P("batch", "head"),
        P("batch", "head"),
        P("batch", "head"),
        P("batch", "head"),
        P("batch", "head"),
        P(),
        P("batch", "head", None, None),
        P("head", None),
        P(),
        P(None, "head"),
        P("head", None, None),
        P(),
        P(),
        P("batch", None, None),
        P(),
        P(),
        P("batch"),
        P("batch"),
        P("head", None, None),
    )
    out_specs = (P("batch", "head"), P("batch", "head", None, None), P("batch", "head"))
    return jax.shard_map(
        on_device, mesh=mesh, in_specs=in_specs, out_specs=out_specs, check_vma=False
    )
```
